32 devices in a mesh: groups: 2 (over y), expert: 4 (over z), head: 2 (over x), pair: 2 (over core).
Axes of the slice: x: 2, y: 2, z: 4, core: 2. Of those that a mesh axis runs over, the one named last changes fastest.
Arguments:
- resid: bfloat16 [1024, 4096], P(('groups', 'expert'), ('head', 'pair')), parts along dimension 0, may hold values from -12 to 12
- query: bfloat16 [1024, 4096], P(('groups', 'expert'), ('head', 'pair')), parts along dimension 0, may hold values from -48 to 48
- keyval: bfloat16 [2, 1024, 512], P(None, ('groups', 'expert'), 'head'), parts along dimension 1, may hold values from -8 to 8
- wo: bfloat16 [4096, 4096], P(('head', 'pair'), 'expert'), may hold values from -0.375 to 0.375
- norm_gain: float32 [4096], replicated, may hold values from 0.1 to 1.9
- w_gate: bfloat16 [4, 4096, 1024], P('expert', None, ('head', 'pair')), may hold values from -0.09375 to 0.09375
- w_up: bfloat16 [4, 4096, 1024], P('expert', None, ('head', 'pair')), may hold values from -0.09375 to 0.09375
- w_down: bfloat16 [4, 1024, 4096], P('expert', None, ('head', 'pair')), may hold values from -0.1875 to 0.1875
- expert_ids: int32 [1024, 2], P(('groups', 'expert')), parts along dimension 0, may hold values from 0 to 3, as said below
- slot_ids: int32 [1024, 2], P(('groups', 'expert')), parts along dimension 0, may hold values from 0 to 127, as said below
- route_weights: float32 [1024, 2], P(('groups', 'expert')), parts along dimension 0, may hold values from 0.1 to 0.6
Outputs:
- attn_hidden: bfloat16 [1024, 4096], P(('groups', 'expert'), ('head', 'pair')), parts along dimension 0
- expert_mix: bfloat16 [1024, 4096], P(('groups', 'expert'), ('head', 'pair')), parts along dimension 0
The draws below stay inside these ranges and needn't reach their ends.
There are 2 independent parts, one for each index of `groups`. The reference program is written for one: setup_inputs(seed, part) draws one part's arguments, and reference() takes and returns one part's arrays. A program takes and returns all parts, laid end to end along the dimension named above; an argument that names none is the same for every part. Nothing has to cross between parts.
Inputs may be any that keep to these rules, and one draw needn't show every extreme that they name: `expert_ids`: each token names 2 different experts. Within each aligned block of 128 tokens no expert is named more than 128 times, and one expert, the same in every block of a draw, is named exactly 128 times in every block. `slot_ids`: within each aligned block of 128 tokens the routes to one expert hold the slots 0 to their count - 1, each once.
All inputs are finite; a program needn't handle non-finite values.
Results may differ from the reference program's by a relative error of at most 0.02.
Values may be sent and summed in bfloat16 or wider, within the bound.
A program may use at most 64 MiB of HBM per device.

```python
import math
import jax
import jax.numpy as jnp
from jax import lax

D = 4096
QUERY_HEADS = 32
KEY_VALUE_HEADS = 4
HEAD_WIDTH = 128
FFE = 1024
TOPK = 2
TOK_DEV = 128
IMAGE_TOKENS = 512
EXPERTS = 4
CAP = 128


def routing_tables(key):
    base_key = jax.random.fold_in(key, 11)
    hot_expert = jax.random.randint(jax.random.fold_in(base_key, 1), (), 0, EXPERTS)
    block_keys = jax.random.split(jax.random.fold_in(base_key, 2), IMAGE_TOKENS // TOK_DEV)
    route_count = TOK_DEV * TOPK

    def one_block(block_key):
        perm_key, count_key, order_key = jax.random.split(block_key, 3)
        order_perm = jax.random.permutation(perm_key, EXPERTS)
        order_perm = (order_perm - order_perm[0] + hot_expert) % EXPERTS
        pair_small = jax.random.randint(count_key, (EXPERTS // 2,), 1, CAP)
        pair_small = pair_small.at[0].set(0)
        pair_counts = jnp.stack([CAP - pair_small, pair_small], axis=1).reshape(EXPERTS).astype(jnp.int32)
        counts = jnp.zeros((EXPERTS,), jnp.int32).at[order_perm].set(pair_counts)
        starts = jnp.cumsum(counts) - counts
        labels = jnp.repeat(jnp.arange(EXPERTS, dtype=jnp.int32), counts, total_repeat_length=route_count)
        slot_vals = jnp.arange(route_count, dtype=jnp.int32) - starts[labels]
        expert_vals = labels.reshape(TOPK, TOK_DEV).T
        slot_vals = slot_vals.reshape(TOPK, TOK_DEV).T
        token_order = jax.random.permutation(order_key, TOK_DEV)
        return (expert_vals[token_order], slot_vals[token_order])
    expert_vals, slot_vals = jax.vmap(one_block)(block_keys)
    return (expert_vals.reshape(IMAGE_TOKENS, TOPK).astype(jnp.int32), slot_vals.reshape(IMAGE_TOKENS, TOPK).astype(jnp.int32))


def draw_expert_ids(key, part):
    return routing_tables(key)[0]


def draw_slot_ids(key, part):
    return routing_tables(key)[1]


def attention_tables(key):
    base_key = jax.random.fold_in(key, 23)
    query_key, key_random_seed, value_random_seed = jax.random.split(base_key, 3)
    queries = 1.5 * jax.random.truncated_normal(query_key, -4.0, 4.0, (IMAGE_TOKENS, QUERY_HEADS * HEAD_WIDTH), jnp.float32)
    every_key_row = 1.5 * jax.random.truncated_normal(key_random_seed, -4.0, 4.0, (IMAGE_TOKENS, KEY_VALUE_HEADS * HEAD_WIDTH), jnp.float32)
    every_value_row = jax.random.truncated_normal(value_random_seed, -4.0, 4.0, (IMAGE_TOKENS, KEY_VALUE_HEADS * HEAD_WIDTH), jnp.float32)
    return (queries, jnp.stack([every_key_row, every_value_row]))


def draw_query(key, part):
    return attention_tables(key)[0].astype(jnp.bfloat16)


def draw_keyval(key, part):
    return attention_tables(key)[1].astype(jnp.bfloat16)


def draw_resid(key, part):
    column_pos = jnp.arange(D, dtype=jnp.float32) / D
    noise_key = jax.random.fold_in(jax.random.fold_in(key, 31), 0)
    base_vals = jax.random.truncated_normal(noise_key, -4.0, 4.0, (IMAGE_TOKENS, D), jnp.float32)
    return (base_vals * (0.6 + 1.2 * column_pos)).astype(jnp.bfloat16)


def block_scale(own_key, dims, shards, low, high):
    level, own = 1.0, jax.random.fold_in(own_key, 6)
    for axis_at, blocks in shards:
        steps = jnp.exp(jax.random.uniform(jax.random.fold_in(own, axis_at), (blocks,), jnp.float32, low / len(shards), high / len(shards)))
        level = level * jnp.repeat(steps, dims[axis_at] // blocks).reshape([-1 if axis == axis_at else 1 for axis in range(len(dims))])
    return level


def centred(own_key, dims, scale, most, cuts=(), held_as=jnp.bfloat16):
    loudness = block_scale(own_key, dims, cuts, -0.22, 0.18) if cuts else 1.0
    result = jax.random.normal(own_key, dims, jnp.float32) * scale * loudness
    return jnp.minimum(jnp.maximum(result, -most), most).astype(held_as)


def setup_inputs(seed: int = 0, part: int = 0) -> dict:
    arg_keys = jax.random.split(jax.random.key(seed), 12)
    own_keys = jax.random.split(jax.random.fold_in(arg_keys[11], part), 12)
    resid = draw_resid(jax.random.fold_in(jax.random.fold_in(arg_keys[11], part), 71), part)
    query = draw_query(jax.random.fold_in(jax.random.fold_in(arg_keys[11], part), 71), part)
    keyval = draw_keyval(jax.random.fold_in(jax.random.fold_in(arg_keys[11], part), 71), part)
    wo = centred(arg_keys[3], (QUERY_HEADS * HEAD_WIDTH, D), (QUERY_HEADS * HEAD_WIDTH // 16) ** -0.5, 0.375, ((0, 4), (1, 4)))
    norm_gain = jnp.clip(1.0 + 0.18 * jax.random.normal(arg_keys[4], (D,), jnp.float32), 0.1, 1.9)
    w_gate = centred(arg_keys[5], (EXPERTS, D, FFE), D ** -0.5, 0.09375, ((0, 4), (2, 4)))
    w_up = centred(arg_keys[6], (EXPERTS, D, FFE), D ** -0.5, 0.09375, ((0, 4), (2, 4)))
    w_down = centred(arg_keys[7], (EXPERTS, FFE, D), FFE ** -0.5, 0.1875, ((0, 4), (2, 4)))
    expert_ids = draw_expert_ids(jax.random.fold_in(jax.random.fold_in(arg_keys[11], part), 71), part)
    slot_ids = draw_slot_ids(jax.random.fold_in(jax.random.fold_in(arg_keys[11], part), 71), part)
    route_weights = jnp.clip(0.1 + 0.5 * jax.random.uniform(own_keys[10], (IMAGE_TOKENS, TOPK), jnp.float32) ** block_scale(own_keys[10], (IMAGE_TOKENS, TOPK), ((0, 4),), -0.2, 0.2), 0.1, 0.6)
    return dict(resid=resid, query=query, keyval=keyval, wo=wo, norm_gain=norm_gain, w_gate=w_gate, w_up=w_up, w_down=w_down, expert_ids=expert_ids, slot_ids=slot_ids, route_weights=route_weights)


norm_eps = 1e-06

def reference(resid, query, keyval, wo, norm_gain, w_gate, w_up, w_down, expert_ids, slot_ids, route_weights):
    heads_per_group = QUERY_HEADS // KEY_VALUE_HEADS
    positions = jnp.arange(IMAGE_TOKENS, dtype=jnp.int32)
    causal = positions[None, :] <= positions[:, None]

    def one_head(head_index):
        kv_index = head_index // heads_per_group
        query_head = lax.dynamic_slice_in_dim(query, head_index * HEAD_WIDTH, HEAD_WIDTH, 1)
        key_head = lax.dynamic_slice_in_dim(keyval[0], kv_index * HEAD_WIDTH, HEAD_WIDTH, 1)
        value_head = lax.dynamic_slice_in_dim(keyval[1], kv_index * HEAD_WIDTH, HEAD_WIDTH, 1)
        scores = jnp.dot(query_head, key_head.T, preferred_element_type=jnp.float32) / math.sqrt(HEAD_WIDTH)
        scores = jnp.where(causal, scores, -jnp.inf)
        row_max = lax.optimization_barrier(jnp.max(scores, axis=1, keepdims=True))
        weights = jnp.where(causal, jnp.exp(scores - row_max), 0.0)
        softmax_total = lax.optimization_barrier(jnp.sum(weights, axis=1, keepdims=True))
        mixed = jnp.dot(weights.astype(jnp.bfloat16), value_head, preferred_element_type=jnp.float32)
        return (mixed / softmax_total).astype(jnp.bfloat16)
    head_outs = lax.map(one_head, jnp.arange(QUERY_HEADS, dtype=jnp.int32))
    heads_out = head_outs.transpose(1, 0, 2).reshape(IMAGE_TOKENS, QUERY_HEADS * HEAD_WIDTH)
    attn_hidden = (resid.astype(jnp.float32) + jnp.dot(heads_out, wo, preferred_element_type=jnp.float32)).astype(jnp.bfloat16)
    hidden_f32 = attn_hidden.astype(jnp.float32)
    mean_square = lax.optimization_barrier(jnp.mean(hidden_f32 * hidden_f32, axis=1, keepdims=True))
    normed = (hidden_f32 * lax.rsqrt(mean_square + norm_eps) * norm_gain).astype(jnp.bfloat16)
    block_count = IMAGE_TOKENS // TOK_DEV
    block_of = (jnp.arange(IMAGE_TOKENS, dtype=jnp.int32) // TOK_DEV)[:, None]
    buffer_row = (expert_ids * (block_count * CAP) + block_of * CAP + slot_ids).astype(jnp.int32)
    slot_rows = jnp.zeros((EXPERTS * block_count * CAP, D), jnp.bfloat16)
    slot_rows = slot_rows.at[buffer_row.reshape(-1)].set(jnp.repeat(normed, TOPK, axis=0))
    slot_rows = slot_rows.reshape(EXPERTS, block_count * CAP, D)

    def one_expert(expert_index):
        slot_block = slot_rows[expert_index]
        gate_val = jnp.dot(slot_block, w_gate[expert_index], preferred_element_type=jnp.float32)
        up_val = jnp.dot(slot_block, w_up[expert_index], preferred_element_type=jnp.float32)
        activated = (jax.nn.silu(gate_val) * up_val).astype(jnp.bfloat16)
        return jnp.dot(activated, w_down[expert_index], preferred_element_type=jnp.float32).astype(jnp.bfloat16)
    expert_out = lax.map(one_expert, jnp.arange(EXPERTS, dtype=jnp.int32)).reshape(EXPERTS * block_count * CAP, D)
    picked = expert_out[buffer_row]
    expert_mix = lax.optimization_barrier(jnp.sum(route_weights[:, :, None] * picked.astype(jnp.float32), axis=1)).astype(jnp.bfloat16)
    return (attn_hidden, expert_mix)
```

```python
import functools
import math

import jax
import jax.numpy as jnp
from jax import lax
from jax.experimental import pallas as pl
from jax.experimental.pallas import tpu as pltpu
from jax.sharding import PartitionSpec as P

D = 4096
QUERY_HEADS = 32
KEY_VALUE_HEADS = 4
HEAD_WIDTH = 128
TOPK = 2


norm_eps = 1e-06


def expert_block(w_gate, w_up, w_down, slot_block):
    gate_val = jnp.einsum("ensd,edf->ensf", slot_block, w_gate, preferred_element_type=jnp.float32)
    up_val = jnp.einsum("ensd,edf->ensf", slot_block, w_up, preferred_element_type=jnp.float32)
    activated = (jax.nn.silu(gate_val) * up_val).astype(jnp.bfloat16)
    all_hidden = lax.all_gather(activated, ("head", "pair"), axis=3, tiled=True)
    return jnp.einsum(
        "ensf,efd->ensd", all_hidden, w_down, preferred_element_type=jnp.float32
    ).astype(jnp.bfloat16)


def slotted_body(
    resid, query, keyval, wo, norm_gain, w_gate, w_up, w_down, expert_ids, slot_ids, route_weights
):
    tok_rows = resid.shape[0]
    feature_cols = resid.shape[1]
    q_local = query.shape[1] // HEAD_WIDTH
    kv_local = keyval.shape[2] // HEAD_WIDTH
    heads_per_group = QUERY_HEADS // KEY_VALUE_HEADS
    query_pos = lax.axis_index("expert") * tok_rows + jnp.arange(tok_rows, dtype=jnp.int32)
    key_head = (
        lax.axis_index("pair") * q_local + jnp.arange(q_local, dtype=jnp.int32)
    ) // heads_per_group
    queries = query.reshape(tok_rows, q_local, HEAD_WIDTH)
    inverse_root = 1.0 / math.sqrt(HEAD_WIDTH)
    shards = lax.all_gather(keyval, "expert", axis=1, tiled=True)
    run_max = jnp.full((tok_rows, q_local), -1e30, jnp.float32)
    count = shards.shape[1]
    keys_here = jnp.take(shards[0].reshape(count, kv_local, HEAD_WIDTH), key_head, axis=1)
    values_here = jnp.take(shards[1].reshape(count, kv_local, HEAD_WIDTH), key_head, axis=1)
    scores = (
        jnp.einsum("thd,uhd->thu", queries, keys_here, preferred_element_type=jnp.float32)
        * inverse_root
    )
    key_pos = jnp.arange(count, dtype=jnp.int32)
    visible = (key_pos[None, :] <= query_pos[:, None])[:, None, :]
    scores = jnp.where(visible, scores, -jnp.inf)
    new_max = jnp.maximum(run_max, jnp.max(scores, axis=2))
    weights = jnp.where(visible, jnp.exp(scores - new_max[:, :, None]), 0.0)
    run_total = jnp.sum(weights, axis=2)
    weighted = jnp.einsum(
        "thu,uhd->thd",
        weights.astype(jnp.bfloat16),
        values_here,
        preferred_element_type=jnp.float32,
    )
    run_max, run_total, weighted = (new_max, run_total, weighted)
    heads_out = (
        (weighted / run_total[:, :, None])
        .astype(jnp.bfloat16)
        .reshape(tok_rows, q_local * HEAD_WIDTH)
    )
    partial_proj = jnp.dot(
        heads_out,
        lax.all_gather(wo, "expert", axis=1, tiled=True),
        preferred_element_type=jnp.float32,
    )
    attn_sum = lax.psum_scatter(
        partial_proj.astype(jnp.bfloat16), ("head", "pair"), scatter_dimension=1, tiled=True
    ).astype(jnp.float32)
    attn_hidden = (resid.astype(jnp.float32) + attn_sum).astype(jnp.bfloat16)
    experts_here = w_gate.shape[0]
    experts_all = experts_here * lax.axis_size("expert")
    capacity = 2 * tok_rows * TOPK // experts_all
    target = expert_ids * capacity + slot_ids
    slot_index = jnp.arange(experts_all * capacity, dtype=jnp.int32)
    placing = jnp.sum(
        (target[None, :, :] == slot_index[:, None, None]).astype(jnp.int32), axis=2
    ).astype(jnp.bfloat16)
    row_floats = attn_hidden.astype(jnp.float32)
    square_sum = lax.psum(jnp.sum(row_floats * row_floats, axis=1), ("head", "pair"))
    mean_square = (square_sum / D)[:, None]
    shard_index = lax.axis_index("head") * lax.axis_size("pair") + lax.axis_index("pair")
    gain_part = lax.dynamic_slice_in_dim(norm_gain, shard_index * feature_cols, feature_cols)
    normed = (row_floats * lax.rsqrt(mean_square + norm_eps) * gain_part).astype(jnp.bfloat16)
    filled = jnp.dot(placing, normed, preferred_element_type=jnp.float32).astype(jnp.bfloat16)
    whole_rows = lax.all_gather(
        lax.all_to_all(
            filled.reshape(experts_all, 1, capacity, normed.shape[1]),
            "expert",
            split_axis=0,
            concat_axis=1,
            tiled=True,
        ),
        ("head", "pair"),
        axis=3,
        tiled=True,
    )
    expert_out = expert_block(w_gate, w_up, w_down, whole_rows)
    returned = lax.all_to_all(expert_out, "expert", split_axis=1, concat_axis=0, tiled=True)
    returned = returned.reshape(experts_all * capacity, feature_cols)
    picked = jnp.take(returned, target.reshape(-1), axis=0).reshape(tok_rows, TOPK, feature_cols)
    expert_mix = jnp.sum(route_weights[:, :, None] * picked.astype(jnp.float32), axis=1).astype(
        jnp.bfloat16
    )
    return (attn_hidden, expert_mix)


MESH = pl.DeviceIdType.MESH


def fused_kernel(
    nz, nx, npair, q_ref, kv_ref, resid_ref, gain_ref, ids_ref, rw_ref, wo_hbm, wg_hbm, wu_hbm, wd_hbm,
    hid_ref, mix_ref,
    wo, wgu, wd, kv_all, ho, pbuf, pin, resid_t, xall, act_all, eo, ret,
    w_sem, self_sem, kv_s, kv_r, rs_s, rs_r, ho_s, ho_r, p_s, p_r, z_s, z_r, x_s, x_r, c_s, c_r, f_s, f_r,
    a_s, a_r, e_s, e_r,
):
    nhp = nx * npair
    g, z = lax.axis_index("groups"), lax.axis_index("expert")
    x, p = lax.axis_index("head"), lax.axis_index("pair")
    hp = x * npair + p
    rows, cols = q_ref.shape
    part_rows = rows // nhp
    hidden = wg_hbm.shape[2]
    heads = cols // HEAD_WIDTH
    f32, bf16 = jnp.float32, jnp.bfloat16

    def at(zt, hpt):
        return (g, zt, hpt // npair, lax.rem(hpt, npair))

    def remote(src, dst, ssem, rsem, dev):
        return pltpu.make_async_remote_copy(
            src_ref=src, dst_ref=dst, send_sem=ssem, recv_sem=rsem, device_id=dev, device_id_type=MESH
        )

    def slab(index):
        return pl.ds(pl.multiple_of(index * part_rows, part_rows), part_rows)

    mine = slab(hp)
    z_others = [lax.rem(z + d, nz) for d in range(1, nz)]
    hp_others = [lax.rem(hp + d, nhp) for d in range(1, nhp)]
    x_dev = (g, z, 1 - x, p)
    c_dev = (g, z, x, 1 - p)
    hp_x = (1 - x) * npair + p
    hp_c = x * npair + 1 - p
    hp_xc = (1 - x) * npair + 1 - p

    weights = [
        pltpu.make_async_copy(wo_hbm, wo, w_sem.at[0]),
        pltpu.make_async_copy(wg_hbm.at[0], wgu.at[:, 0:hidden], w_sem.at[1]),
        pltpu.make_async_copy(wu_hbm.at[0], wgu.at[:, hidden : 2 * hidden], w_sem.at[2]),
        pltpu.make_async_copy(wd_hbm.at[0], wd, w_sem.at[3]),
    ]
    for copy in weights:
        copy.start()
    kv_all[z] = kv_ref[:, :, pl.ds(pl.multiple_of(p * HEAD_WIDTH, HEAD_WIDTH), HEAD_WIDTH)]

    barrier = pltpu.get_barrier_semaphore()
    for dz in range(nz):
        for dh in range(nhp):
            if dz or dh:
                pl.semaphore_signal(
                    barrier,
                    inc=1,
                    device_id=at(lax.rem(z + dz, nz), lax.rem(hp + dh, nhp)),
                    device_id_type=MESH,
                )
    pl.semaphore_wait(barrier, nz * nhp - 1)

    def kv_copy(i, zt):
        return remote(kv_all.at[z], kv_all.at[z], kv_s.at[i], kv_r.at[z], at(zt, hp))

    for d in range(nz - 1, 0, -1):
        @pl.when(z + d < nz)
        def _():
            kv_copy(d, lax.rem(z + d, nz)).start()

    def resid_copy(j):
        return remote(resid_ref.at[pl.ds(j * part_rows, part_rows)], resid_t.at[z], rs_s.at[j], rs_r.at[z], at(hp, j))

    for j in range(nhp):
        is_self = jnp.logical_and(z == hp, hp == j)

        @pl.when(jnp.logical_not(is_self))
        def _():
            resid_copy(j).start()

        @pl.when(is_self)
        def _():
            resid_t[z] = resid_ref[pl.ds(j * part_rows, part_rows), :]

    scale = 1.0 / math.sqrt(HEAD_WIDTH)
    for n in range(nz):
        @pl.when(z == n)
        def _():
            for b in range(n):
                remote(kv_all.at[b], kv_all.at[b], kv_s.at[0], kv_r.at[b], at(b, hp)).wait_recv()
            count = (n + 1) * rows
            keys = kv_all[0 : n + 1, 0].reshape(count, HEAD_WIDTH)
            values = kv_all[0 : n + 1, 1].reshape(count, HEAD_WIDTH)
            row = lax.broadcasted_iota(jnp.int32, (rows, count), 0) + n * rows
            col = lax.broadcasted_iota(jnp.int32, (rows, count), 1)
            visible = col <= row
            for h in range(heads):
                span = slice(h * HEAD_WIDTH, (h + 1) * HEAD_WIDTH)
                scores = lax.dot_general(
                    q_ref[:, span], keys, (((1,), (1,)), ((), ())), preferred_element_type=f32
                )
                scores = jnp.where(visible, scores * scale, -jnp.inf)
                probs = jnp.exp(scores - jnp.max(scores, axis=1, keepdims=True))
                total = jnp.sum(probs, axis=1, keepdims=True)
                mixed = jnp.dot(probs.astype(bf16), values, preferred_element_type=f32)
                ho[n, :, span] = (mixed / total).astype(bf16)

    def ho_copy(i):
        return remote(ho.at[z], ho.at[z], ho_s.at[i], ho_r.at[z], at(z_others[i], hp))

    for i in range(nz - 1):
        ho_copy(i).start()
    weights[0].wait()

    def p_copy(b, i):
        return remote(pbuf.at[b, slab(hp_others[i])], pin.at[b, hp], p_s.at[b, i], p_r.at[b, hp], at(z, hp_others[i]))

    def z_copy(b, i):
        return remote(
            xall.at[b, z, mine], xall.at[b, z, mine], z_s.at[b, i], z_r.at[b, z], at(z_others[i], hp)
        )

    def group_copy(b, owner, ssem, rsem, dev):
        ref = xall.at[b, :, slab(owner)]
        return remote(ref, ref, ssem.at[b], rsem.at[b], dev)

    def a_copy(b, i):
        return remote(act_all.at[b, hp], act_all.at[b, hp], a_s.at[b, i], a_r.at[b, hp], at(z, hp_others[i]))

    def e_copy(b):
        return remote(eo.at[b], ret.at[z], e_s.at[b], e_r.at[z], at(b, hp))

    def project(b):
        @pl.when(z != b)
        def _():
            remote(ho.at[b], ho.at[b], ho_s.at[0], ho_r.at[b], at(b, hp)).wait_recv()

        pbuf[b] = jnp.dot(ho[b], wo[...], preferred_element_type=f32).astype(bf16)
        for i in range(nhp - 1):
            p_copy(b, i).start()

    def add_up(b):
        @pl.when(jnp.logical_not(jnp.logical_and(z == b, hp == z)))
        def _():
            remote(
                resid_ref.at[pl.ds(0, part_rows)], resid_t.at[b], rs_s.at[0], rs_r.at[b], at(b, z)
            ).wait_recv()

        for other in hp_others:
            remote(pbuf.at[b, mine], pin.at[b, other], p_s.at[b, 0], p_r.at[b, other], at(z, other)).wait_recv()
        total = pbuf[b, mine, :].astype(f32)
        for other in hp_others:
            total = total + pin[b, other].astype(f32)
        xall[b, z, mine, :] = (resid_t[b].astype(f32) + total).astype(bf16)
        for i in range(nz - 1):
            z_copy(b, i).start()

    def spread(b):
        for other in z_others:
            ref = xall.at[b, other, mine]
            remote(ref, ref, z_s.at[b, 0], z_r.at[b, other], at(other, hp)).wait_recv()
        group_copy(b, hp, x_s, x_r, x_dev).start()
        group_copy(b, hp, c_s, c_r, c_dev).start()

    def hidden_units(b):
        group_copy(b, hp_x, x_s, x_r, x_dev).wait_recv()
        group_copy(b, hp_x, f_s, f_r, c_dev).start()
        group_copy(b, hp_c, c_s, c_r, c_dev).wait_recv()
        group_copy(b, hp_xc, f_s, f_r, c_dev).wait_recv()
        square = jnp.zeros((rows, 1), f32)
        for e in range(nz):
            part = xall[b, e].astype(f32)
            square = square + jnp.sum(part * part, axis=1, keepdims=True)
        root = lax.rsqrt(square / D + norm_eps)
        both = jnp.zeros((rows, 2 * hidden), f32)
        for e in range(nz):
            normed = (xall[b, e].astype(f32) * root * gain_ref[e]).astype(bf16)
            both = both + jnp.dot(normed, wgu[e * cols : (e + 1) * cols, :], preferred_element_type=f32)
        gate, up = both[:, :hidden], both[:, hidden:]
        act_all[b, hp] = (gate / (1.0 + jnp.exp(-gate)) * up).astype(bf16)
        for i in range(nhp - 1):
            a_copy(b, i).start()

    def down(b):
        for other in hp_others:
            ref = act_all.at[b, other]
            remote(ref, ref, a_s.at[b, 0], a_r.at[b, other], at(z, other)).wait_recv()
        total = jnp.zeros((rows, cols), f32)
        for j in range(nhp):
            total = total + jnp.dot(
                act_all[b, j], wd[j * hidden : (j + 1) * hidden, :], preferred_element_type=f32
            )
        eo[b] = total.astype(bf16)

        @pl.when(z != b)
        def _():
            e_copy(b).start()

    for step in range(nz + 4):
        if step < nz:
            project(step)
        if 0 <= step - 1 < nz:
            add_up(step - 1)
        if 0 <= step - 2 < nz:
            spread(step - 2)
        if 0 <= step - 3 < nz:
            if step == 3:
                weights[1].wait()
                weights[2].wait()
            hidden_units(step - 3)
        if 0 <= step - 4 < nz:
            if step == 4:
                weights[3].wait()
            down(step - 4)

    hid_ref[...] = xall[z, hp]
    mix = route_share(ids_ref, rw_ref, z) * eo[z].astype(f32)
    for other in z_others:
        remote(eo.at[0], ret.at[other], e_s.at[0], e_r.at[other], at(other, hp)).wait_recv()
        mix = mix + route_share(ids_ref, rw_ref, other) * ret[other].astype(f32)
    mix_ref[...] = mix.astype(bf16)

    for d in range(1, nz):
        @pl.when(z + d < nz)
        def _():
            kv_copy(d, lax.rem(z + d, nz)).wait_send()

    for j in range(nhp):
        @pl.when(jnp.logical_not(jnp.logical_and(z == hp, hp == j)))
        def _():
            resid_copy(j).wait_send()

    for i in range(nz - 1):
        ho_copy(i).wait_send()
    for b in range(nz):
        for i in range(nhp - 1):
            p_copy(b, i).wait_send()
            a_copy(b, i).wait_send()
        for i in range(nz - 1):
            z_copy(b, i).wait_send()
        group_copy(b, hp, x_s, x_r, x_dev).wait_send()
        group_copy(b, hp, c_s, c_r, c_dev).wait_send()
        group_copy(b, hp_x, f_s, f_r, c_dev).wait_send()

        @pl.when(z != b)
        def _():
            e_copy(b).wait_send()


def route_share(ids_ref, rw_ref, expert):
    return jnp.sum(jnp.where(ids_ref[...] == expert, rw_ref[...], 0.0), axis=1, keepdims=True)


def fused_body(
    resid, query, keyval, wo, norm_gain, w_gate, w_up, w_down, expert_ids, slot_ids, route_weights
):
    nz, nx, npair = (lax.axis_size(name) for name in ("expert", "head", "pair"))
    nhp = nx * npair
    rows, cols = resid.shape
    part_rows = rows // nhp
    hidden = w_gate.shape[2]
    bf16 = jnp.bfloat16
    dma = pltpu.SemaphoreType.DMA
    vmem = pl.BlockSpec(memory_space=pltpu.VMEM)
    anywhere = pl.BlockSpec(memory_space=pl.ANY)
    out = jax.ShapeDtypeStruct((rows, cols), bf16)
    tokens = nz * rows
    flops = 2 * tokens * (wo.shape[0] * cols + 2 * w_gate.shape[1] * hidden + w_down.shape[1] * cols)
    return pl.pallas_call(
        functools.partial(fused_kernel, nz, nx, npair),
        out_shape=(out, out),
        in_specs=[vmem] * 6 + [anywhere] * 4,
        out_specs=(vmem, vmem),
        scratch_shapes=[
            pltpu.VMEM(wo.shape, bf16),
            pltpu.VMEM((w_gate.shape[1], 2 * hidden), bf16),
            pltpu.VMEM(w_down.shape[1:], bf16),
            pltpu.VMEM((nz, 2, rows, HEAD_WIDTH), bf16),
            pltpu.VMEM((nz, rows, cols), bf16),
            pltpu.VMEM((nz, rows, cols), bf16),
            pltpu.VMEM((nz, nhp, part_rows, cols), bf16),
            pltpu.VMEM((nz, part_rows, cols), bf16),
            pltpu.VMEM((nz, nz, rows, cols), bf16),
            pltpu.VMEM((nz, nhp, rows, hidden), bf16),
            pltpu.VMEM((nz, rows, cols), bf16),
            pltpu.VMEM((nz, rows, cols), bf16),
            dma((4,)),
            dma((1,)),
            dma((nz,)), dma((nz,)),
            dma((nhp,)), dma((nz,)),
            dma((nz,)), dma((nz,)),
            dma((nz, nhp)), dma((nz, nhp)),
            dma((nz, nz)), dma((nz, nz)),
            dma((nz,)), dma((nz,)),
            dma((nz,)), dma((nz,)),
            dma((nz,)), dma((nz,)),
            dma((nz, nhp)), dma((nz, nhp)),
            dma((nz,)), dma((nz,)),
        ],
        compiler_params=pltpu.CompilerParams(
            collective_id=0, has_side_effects=True, vmem_limit_bytes=48 * 1024 * 1024
        ),
        cost_estimate=pl.CostEstimate(
            flops=flops, bytes_accessed=2 * (wo.size + 3 * w_gate.size), transcendentals=0
        ),
    )(
        query, keyval, resid, norm_gain.reshape(nz, 1, cols), expert_ids, route_weights, wo, w_gate, w_up, w_down
    )


def body(
    resid, query, keyval, wo, norm_gain, w_gate, w_up, w_down, expert_ids, slot_ids, route_weights
):
    args = (resid, query, keyval, wo, norm_gain, w_gate, w_up, w_down, expert_ids, slot_ids, route_weights)
    nz, nx, npair = (lax.axis_size(name) for name in ("expert", "head", "pair"))
    rows = resid.shape[0]
    capacity = 2 * rows * TOPK // (w_gate.shape[0] * nz)
    dense = (
        capacity == rows
        and w_gate.shape[0] == 1
        and nz == nx * npair
        and nx == 2
        and npair == 2
        and query.shape[1] // HEAD_WIDTH == QUERY_HEADS // KEY_VALUE_HEADS
        and rows % (16 * nx * npair) == 0
    )
    return fused_body(*args) if dense else slotted_body(*args)


def solution(mesh):
    return jax.shard_map(
        body,
        mesh=mesh,
        in_specs=(
            P(("groups", "expert"), ("head", "pair")),
            P(("groups", "expert"), ("head", "pair")),
            P(None, ("groups", "expert"), "head"),
            P(("head", "pair"), "expert"),
            P(),
            P("expert", None, ("head", "pair")),
            P("expert", None, ("head", "pair")),
            P("expert", None, ("head", "pair")),
            P(("groups", "expert"), None),
            P(("groups", "expert"), None),
            P(("groups", "expert"), None),
        ),
        out_specs=(
            P(("groups", "expert"), ("head", "pair")),
            P(("groups", "expert"), ("head", "pair")),
        ),
        check_vma=False,
    )
```

```python
import functools
import math

import jax
import jax.numpy as jnp
from jax import lax
from jax.experimental import pallas as pl
from jax.experimental.pallas import tpu as pltpu
from jax.sharding import PartitionSpec as P

D = 4096
QUERY_HEADS = 32
KEY_VALUE_HEADS = 4
HEAD_WIDTH = 128
TOPK = 2


norm_eps = 1e-06


def expert_block(w_gate, w_up, w_down, slot_block):
    gate_val = jnp.einsum("ensd,edf->ensf", slot_block, w_gate, preferred_element_type=jnp.float32)
    up_val = jnp.einsum("ensd,edf->ensf", slot_block, w_up, preferred_element_type=jnp.float32)
    activated = (jax.nn.silu(gate_val) * up_val).astype(jnp.bfloat16)
    all_hidden = lax.all_gather(activated, ("head", "pair"), axis=3, tiled=True)
    return jnp.einsum(
        "ensf,efd->ensd", all_hidden, w_down, preferred_element_type=jnp.float32
    ).astype(jnp.bfloat16)


def slotted_body(
    resid, query, keyval, wo, norm_gain, w_gate, w_up, w_down, expert_ids, slot_ids, route_weights
):
    tok_rows = resid.shape[0]
    feature_cols = resid.shape[1]
    q_local = query.shape[1] // HEAD_WIDTH
    kv_local = keyval.shape[2] // HEAD_WIDTH
    heads_per_group = QUERY_HEADS // KEY_VALUE_HEADS
    query_pos = lax.axis_index("expert") * tok_rows + jnp.arange(tok_rows, dtype=jnp.int32)
    key_head = (
        lax.axis_index("pair") * q_local + jnp.arange(q_local, dtype=jnp.int32)
    ) // heads_per_group
    queries = query.reshape(tok_rows, q_local, HEAD_WIDTH)
    inverse_root = 1.0 / math.sqrt(HEAD_WIDTH)
    shards = lax.all_gather(keyval, "expert", axis=1, tiled=True)
    run_max = jnp.full((tok_rows, q_local), -1e30, jnp.float32)
    count = shards.shape[1]
    keys_here = jnp.take(shards[0].reshape(count, kv_local, HEAD_WIDTH), key_head, axis=1)
    values_here = jnp.take(shards[1].reshape(count, kv_local, HEAD_WIDTH), key_head, axis=1)
    scores = (
        jnp.einsum("thd,uhd->thu", queries, keys_here, preferred_element_type=jnp.float32)
        * inverse_root
    )
    key_pos = jnp.arange(count, dtype=jnp.int32)
    visible = (key_pos[None, :] <= query_pos[:, None])[:, None, :]
    scores = jnp.where(visible, scores, -jnp.inf)
    new_max = jnp.maximum(run_max, jnp.max(scores, axis=2))
    weights = jnp.where(visible, jnp.exp(scores - new_max[:, :, None]), 0.0)
    run_total = jnp.sum(weights, axis=2)
    weighted = jnp.einsum(
        "thu,uhd->thd",
        weights.astype(jnp.bfloat16),
        values_here,
        preferred_element_type=jnp.float32,
    )
    run_max, run_total, weighted = (new_max, run_total, weighted)
    heads_out = (
        (weighted / run_total[:, :, None])
        .astype(jnp.bfloat16)
        .reshape(tok_rows, q_local * HEAD_WIDTH)
    )
    partial_proj = jnp.dot(
        heads_out,
        lax.all_gather(wo, "expert", axis=1, tiled=True),
        preferred_element_type=jnp.float32,
    )
    attn_sum = lax.psum_scatter(
        partial_proj.astype(jnp.bfloat16), ("head", "pair"), scatter_dimension=1, tiled=True
    ).astype(jnp.float32)
    attn_hidden = (resid.astype(jnp.float32) + attn_sum).astype(jnp.bfloat16)
    experts_here = w_gate.shape[0]
    experts_all = experts_here * lax.axis_size("expert")
    capacity = 2 * tok_rows * TOPK // experts_all
    target = expert_ids * capacity + slot_ids
    slot_index = jnp.arange(experts_all * capacity, dtype=jnp.int32)
    placing = jnp.sum(
        (target[None, :, :] == slot_index[:, None, None]).astype(jnp.int32), axis=2
    ).astype(jnp.bfloat16)
    row_floats = attn_hidden.astype(jnp.float32)
    square_sum = lax.psum(jnp.sum(row_floats * row_floats, axis=1), ("head", "pair"))
    mean_square = (square_sum / D)[:, None]
    shard_index = lax.axis_index("head") * lax.axis_size("pair") + lax.axis_index("pair")
    gain_part = lax.dynamic_slice_in_dim(norm_gain, shard_index * feature_cols, feature_cols)
    normed = (row_floats * lax.rsqrt(mean_square + norm_eps) * gain_part).astype(jnp.bfloat16)
    filled = jnp.dot(placing, normed, preferred_element_type=jnp.float32).astype(jnp.bfloat16)
    whole_rows = lax.all_gather(
        lax.all_to_all(
            filled.reshape(experts_all, 1, capacity, normed.shape[1]),
            "expert",
            split_axis=0,
            concat_axis=1,
            tiled=True,
        ),
        ("head", "pair"),
        axis=3,
        tiled=True,
    )
    expert_out = expert_block(w_gate, w_up, w_down, whole_rows)
    returned = lax.all_to_all(expert_out, "expert", split_axis=1, concat_axis=0, tiled=True)
    returned = returned.reshape(experts_all * capacity, feature_cols)
    picked = jnp.take(returned, target.reshape(-1), axis=0).reshape(tok_rows, TOPK, feature_cols)
    expert_mix = jnp.sum(route_weights[:, :, None] * picked.astype(jnp.float32), axis=1).astype(
        jnp.bfloat16
    )
    return (attn_hidden, expert_mix)


MESH = pl.DeviceIdType.MESH


def fused_kernel(
    nz, nx, npair, q_hbm, kv_hbm, resid_hbm, gain_hbm, ids_hbm, rw_hbm, wo_hbm, wg_hbm, wu_hbm, wd_hbm,
    hid_ref, mix_ref,
    q_ref, gain_ref, ids_ref, rw_ref,
    wo, wgu, wd, kv_all, ho, pbuf, pin, resid_t, xall, act_all, eo, ret,
    w_sem, in_sem, kv_s, kv_r, rs_s, rs_r, ho_s, ho_r, p_s, p_r, z_s, z_r, x_s, x_r, c_s, c_r, f_s, f_r,
    a_s, a_r, e_s, e_r,
):
    nhp = nx * npair
    g, z = lax.axis_index("groups"), lax.axis_index("expert")
    x, p = lax.axis_index("head"), lax.axis_index("pair")
    hp = x * npair + p
    rows, cols = q_ref.shape
    part_rows = rows // nhp
    hidden = wg_hbm.shape[2]
    heads = cols // HEAD_WIDTH
    half = cols // 2
    f32, bf16 = jnp.float32, jnp.bfloat16

    def at(zt, hpt):
        return (g, zt, hpt // npair, lax.rem(hpt, npair))

    def remote(src, dst, ssem, rsem, dev):
        return pltpu.make_async_remote_copy(
            src_ref=src, dst_ref=dst, send_sem=ssem, recv_sem=rsem, device_id=dev, device_id_type=MESH
        )

    def same(ref, ssem, rsem, dev):
        return remote(ref, ref, ssem, rsem, dev)

    def slab(index):
        return pl.ds(pl.multiple_of(index * part_rows, part_rows), part_rows)

    mine = slab(hp)
    z_others = [lax.rem(z + d, nz) for d in range(1, nz)]
    hp_others = [lax.rem(hp + d, nhp) for d in range(1, nhp)]
    right_ok, left_ok = z + 1 < nz, z > 0
    right, left = lax.rem(z + 1, nz), lax.rem(z + nz - 1, nz)
    x_dev = (g, z, 1 - x, p)
    c_dev = (g, z, x, 1 - p)
    hp_x = (1 - x) * npair + p
    hp_c = x * npair + 1 - p
    hp_xc = (1 - x) * npair + 1 - p

    key_cols = pl.ds(pl.multiple_of(p * HEAD_WIDTH, HEAD_WIDTH), HEAD_WIDTH)
    small = [
        pltpu.make_async_copy(kv_hbm.at[:, :, key_cols], kv_all.at[z], in_sem.at[0]),
        pltpu.make_async_copy(q_hbm, q_ref, in_sem.at[1]),
        pltpu.make_async_copy(gain_hbm, gain_ref, in_sem.at[2]),
        pltpu.make_async_copy(ids_hbm, ids_ref, in_sem.at[3]),
        pltpu.make_async_copy(rw_hbm, rw_ref, in_sem.at[4]),
    ]
    weights = [
        pltpu.make_async_copy(wo_hbm, wo, w_sem.at[0]),
        pltpu.make_async_copy(wg_hbm.at[0], wgu.at[:, 0:hidden], w_sem.at[1]),
        pltpu.make_async_copy(wu_hbm.at[0], wgu.at[:, hidden : 2 * hidden], w_sem.at[2]),
        pltpu.make_async_copy(wd_hbm.at[0], wd, w_sem.at[3]),
    ]
    for copy in small + weights:
        copy.start()

    barrier = pltpu.get_barrier_semaphore()
    for dz in range(nz):
        for dh in range(nhp):
            if dz or dh:
                pl.semaphore_signal(
                    barrier,
                    inc=1,
                    device_id=at(lax.rem(z + dz, nz), lax.rem(hp + dh, nhp)),
                    device_id_type=MESH,
                )
    pl.semaphore_wait(barrier, nz * nhp - 1)

    def kv_copy(b):
        return same(kv_all.at[b], kv_s.at[b], kv_r.at[b], at(right, hp))

    small[0].wait()

    @pl.when(right_ok)
    def _():
        kv_copy(z).start()

    def resid_copy(j):
        return remote(resid_hbm.at[pl.ds(j * part_rows, part_rows)], resid_t.at[z], rs_s.at[j], rs_r.at[z], at(hp, j))

    own_resid = pltpu.make_async_copy(resid_hbm.at[mine], resid_t.at[z], in_sem.at[5])
    for j in range(nhp):
        is_self = jnp.logical_and(z == hp, hp == j)

        @pl.when(jnp.logical_not(is_self))
        def _():
            resid_copy(j).start()

    @pl.when(z == hp)
    def _():
        own_resid.start()

    for copy in small[1:]:
        copy.wait()

    def ho_copy(b, part, way, dev):
        ref = ho.at[b, :, part * half : (part + 1) * half]
        return same(ref, ho_s.at[b, part, way], ho_r.at[b, part], at(dev, hp))

    scale = 1.0 / math.sqrt(HEAD_WIDTH)
    for n in range(nz):
        @pl.when(z == n)
        def _():
            for b in range(n - 1, -1, -1):
                kv_copy(b).wait_recv()
                if n + 1 < nz:
                    kv_copy(b).start()
            count = (n + 1) * rows
            keys = kv_all[0 : n + 1, 0].reshape(count, HEAD_WIDTH)
            values = kv_all[0 : n + 1, 1].reshape(count, HEAD_WIDTH)
            row = lax.broadcasted_iota(jnp.int32, (rows, count), 0) + n * rows
            col = lax.broadcasted_iota(jnp.int32, (rows, count), 1)
            visible = col <= row
            for h in range(heads):
                span = slice(h * HEAD_WIDTH, (h + 1) * HEAD_WIDTH)
                scores = lax.dot_general(
                    q_ref[:, span], keys, (((1,), (1,)), ((), ())), preferred_element_type=f32
                )
                scores = jnp.where(visible, scores * scale, -jnp.inf)
                probs = jnp.exp(scores - jnp.max(scores, axis=1, keepdims=True))
                total = jnp.sum(probs, axis=1, keepdims=True)
                mixed = jnp.dot(probs.astype(bf16), values, preferred_element_type=f32)
                ho[n, :, span] = (mixed / total).astype(bf16)
                if h % (heads // 2) == heads // 2 - 1:
                    part = h // (heads // 2)
                    if n + 1 < nz:
                        ho_copy(n, part, 0, n + 1).start()
                    if n > 0:
                        ho_copy(n, part, 1, n - 1).start()

    def p_copy(b, i):
        return remote(pbuf.at[b, slab(hp_others[i])], pin.at[b, hp], p_s.at[b, i], p_r.at[b, hp], at(z, hp_others[i]))

    def z_copy(b, e, way, dev):
        return same(xall.at[b, e, mine], z_s.at[b, e, way], z_r.at[b, e], at(dev, hp))

    def x_copy(b, e, owner):
        return same(xall.at[b, e, slab(owner)], x_s.at[b, e], x_r.at[b, e], x_dev)

    def c_copy(b, e, owner):
        return same(xall.at[b, e, slab(owner)], c_s.at[b, e], c_r.at[b, e], c_dev)

    def f_copy(b, e, owner):
        return same(xall.at[b, e, slab(owner)], f_s.at[b, e], f_r.at[b, e], c_dev)

    def a_copy(b, i):
        return remote(act_all.at[b, hp], act_all.at[b, hp], a_s.at[b, i], a_r.at[b, hp], at(z, hp_others[i]))

    def e_copy(b):
        return remote(eo.at[b], ret.at[z], e_s.at[b], e_r.at[z], at(b, hp))

    def project(b):
        pbuf[b] = jnp.dot(ho[b], wo[...], preferred_element_type=f32).astype(bf16)
        for i in range(nhp - 1):
            p_copy(b, i).start()

    def heads_hop(d):
        for part in range(2):
            @pl.when(z >= d)
            def _():
                ho_copy(z - d, part, 0, right).wait_recv()

            @pl.when(jnp.logical_and(z >= d, right_ok))
            def _():
                ho_copy(z - d, part, 0, right).start()

            @pl.when(z + d < nz)
            def _():
                ho_copy(z + d, part, 1, left).wait_recv()

            @pl.when(jnp.logical_and(z + d < nz, left_ok))
            def _():
                ho_copy(z + d, part, 1, left).start()

        @pl.when(z >= d)
        def _():
            project(z - d)

        @pl.when(z + d < nz)
        def _():
            project(z + d)

    def add_up(b):
        @pl.when(jnp.logical_not(jnp.logical_and(z == b, hp == z)))
        def _():
            remote(
                resid_hbm.at[pl.ds(0, part_rows)], resid_t.at[b], rs_s.at[0], rs_r.at[b], at(b, z)
            ).wait_recv()

        @pl.when(jnp.logical_and(z == b, hp == z))
        def _():
            own_resid.wait()

        for other in hp_others:
            remote(pbuf.at[b, mine], pin.at[b, other], p_s.at[b, 0], p_r.at[b, other], at(z, other)).wait_recv()
        total = pbuf[b, mine, :].astype(f32)
        for other in hp_others:
            total = total + pin[b, other].astype(f32)
        xall[b, z, mine, :] = (resid_t[b].astype(f32) + total).astype(bf16)

        @pl.when(right_ok)
        def _():
            z_copy(b, z, 0, right).start()

        @pl.when(left_ok)
        def _():
            z_copy(b, z, 1, left).start()

        x_copy(b, z, hp).start()
        c_copy(b, z, hp).start()

    def spread(b, d):
        @pl.when(z >= d)
        def _():
            z_copy(b, z - d, 0, right).wait_recv()

        @pl.when(jnp.logical_and(z >= d, right_ok))
        def _():
            z_copy(b, z - d, 0, right).start()

        @pl.when(z + d < nz)
        def _():
            z_copy(b, z + d, 1, left).wait_recv()

        @pl.when(jnp.logical_and(z + d < nz, left_ok))
        def _():
            z_copy(b, z + d, 1, left).start()

        @pl.when(z >= d)
        def _():
            x_copy(b, z - d, hp).start()
            c_copy(b, z - d, hp).start()

        @pl.when(z + d < nz)
        def _():
            x_copy(b, z + d, hp).start()
            c_copy(b, z + d, hp).start()

    def pass_on(b):
        for e in range(nz):
            x_copy(b, e, hp_x).wait_recv()
            f_copy(b, e, hp_x).start()

    def hidden_units(b):
        for e in range(nz):
            c_copy(b, e, hp_c).wait_recv()
            f_copy(b, e, hp_xc).wait_recv()
        square = jnp.zeros((rows, 1), f32)
        for e in range(nz):
            part = xall[b, e].astype(f32)
            square = square + jnp.sum(part * part, axis=1, keepdims=True)
        root = lax.rsqrt(square / D + norm_eps)
        both = jnp.zeros((rows, 2 * hidden), f32)
        for e in range(nz):
            normed = (xall[b, e].astype(f32) * root * gain_ref[e]).astype(bf16)
            both = both + jnp.dot(normed, wgu[e * cols : (e + 1) * cols, :], preferred_element_type=f32)
        gate, up = both[:, :hidden], both[:, hidden:]
        act_all[b, hp] = (gate / (1.0 + jnp.exp(-gate)) * up).astype(bf16)
        for i in range(nhp - 1):
            a_copy(b, i).start()

    def down(b):
        for other in hp_others:
            ref = act_all.at[b, other]
            remote(ref, ref, a_s.at[b, 0], a_r.at[b, other], at(z, other)).wait_recv()
        total = jnp.zeros((rows, cols), f32)
        for j in range(nhp):
            total = total + jnp.dot(
                act_all[b, j], wd[j * hidden : (j + 1) * hidden, :], preferred_element_type=f32
            )
        eo[b] = total.astype(bf16)

        @pl.when(z != b)
        def _():
            e_copy(b).start()

    order = sorted(range(nz), key=lambda b: max(b, nz - 1 - b))
    first, last = order[: nz // 2], order[nz // 2 :]
    weights[0].wait()
    project(z)
    for d in range(1, nz - 1):
        heads_hop(d)
    for b in first:
        add_up(b)
    heads_hop(nz - 1)
    for b in first:
        spread(b, 1)
    for b in last:
        add_up(b)
    for d in range(2, nz):
        for b in first:
            spread(b, d)
        for b in last:
            spread(b, d - 1)
    pass_on(first[0])
    for b in last:
        spread(b, nz - 1)
    weights[1].wait()
    weights[2].wait()
    weights[3].wait()
    for i in range(nz + 1):
        if i + 1 < nz:
            pass_on(order[i + 1])
        if i < nz:
            hidden_units(order[i])
        if i >= 1:
            down(order[i - 1])

    hid_ref[...] = xall[z, hp]
    diagonal = lax.broadcasted_iota(jnp.int32, (rows, rows), 0) == lax.broadcasted_iota(
        jnp.int32, (rows, rows), 1
    )

    def route_share(expert):
        shares = jnp.sum(jnp.where(ids_ref[...] == expert, rw_ref[...], 0.0), axis=0, keepdims=True)
        return jnp.sum(jnp.where(diagonal, shares, 0.0), axis=1, keepdims=True)

    mix = route_share(z) * eo[z].astype(f32)
    for other in z_others:
        remote(eo.at[0], ret.at[other], e_s.at[0], e_r.at[other], at(other, hp)).wait_recv()
        mix = mix + route_share(other) * ret[other].astype(f32)
    mix_ref[...] = mix.astype(bf16)

    for j in range(nhp):
        @pl.when(jnp.logical_not(jnp.logical_and(z == hp, hp == j)))
        def _():
            resid_copy(j).wait_send()

    for b in range(nz):
        @pl.when(jnp.logical_and(z >= b, right_ok))
        def _():
            kv_copy(b).wait_send()
            for part in range(2):
                ho_copy(b, part, 0, right).wait_send()

        @pl.when(jnp.logical_and(z <= b, left_ok))
        def _():
            for part in range(2):
                ho_copy(b, part, 1, left).wait_send()

        for i in range(nhp - 1):
            p_copy(b, i).wait_send()
            a_copy(b, i).wait_send()
        for e in range(nz):
            @pl.when(jnp.logical_and(z >= e, right_ok))
            def _():
                z_copy(b, e, 0, right).wait_send()

            @pl.when(jnp.logical_and(z <= e, left_ok))
            def _():
                z_copy(b, e, 1, left).wait_send()

            x_copy(b, e, hp).wait_send()
            c_copy(b, e, hp).wait_send()
            f_copy(b, e, hp_x).wait_send()

        @pl.when(z != b)
        def _():
            e_copy(b).wait_send()


def fused_body(
    resid, query, keyval, wo, norm_gain, w_gate, w_up, w_down, expert_ids, slot_ids, route_weights
):
    nz, nx, npair = (lax.axis_size(name) for name in ("expert", "head", "pair"))
    nhp = nx * npair
    rows, cols = resid.shape
    part_rows = rows // nhp
    hidden = w_gate.shape[2]
    bf16 = jnp.bfloat16
    dma = pltpu.SemaphoreType.DMA
    vmem = pl.BlockSpec(memory_space=pltpu.VMEM)
    anywhere = pl.BlockSpec(memory_space=pl.ANY)
    out = jax.ShapeDtypeStruct((rows, cols), bf16)
    tokens = nz * rows
    flops = 2 * tokens * (wo.shape[0] * cols + 2 * w_gate.shape[1] * hidden + w_down.shape[1] * cols)
    return pl.pallas_call(
        functools.partial(fused_kernel, nz, nx, npair),
        out_shape=(out, out),
        in_specs=[anywhere] * 10,
        out_specs=(vmem, vmem),
        scratch_shapes=[
            pltpu.VMEM((rows, cols), bf16),
            pltpu.VMEM((nz, 1, cols), jnp.float32),
            pltpu.VMEM((TOPK, rows), jnp.int32),
            pltpu.VMEM((TOPK, rows), jnp.float32),
            pltpu.VMEM(wo.shape, bf16),
            pltpu.VMEM((w_gate.shape[1], 2 * hidden), bf16),
            pltpu.VMEM(w_down.shape[1:], bf16),
            pltpu.VMEM((nz, 2, rows, HEAD_WIDTH), bf16),
            pltpu.VMEM((nz, rows, cols), bf16),
            pltpu.VMEM((nz, rows, cols), bf16),
            pltpu.VMEM((nz, nhp, part_rows, cols), bf16),
            pltpu.VMEM((nz, part_rows, cols), bf16),
            pltpu.VMEM((nz, nz, rows, cols), bf16),
            pltpu.VMEM((nz, nhp, rows, hidden), bf16),
            pltpu.VMEM((nz, rows, cols), bf16),
            pltpu.VMEM((nz, rows, cols), bf16),
            dma((4,)),
            dma((6,)),
            dma((nz,)), dma((nz,)),
            dma((nhp,)), dma((nz,)),
            dma((nz, 2, 2)), dma((nz, 2)),
            dma((nz, nhp)), dma((nz, nhp)),
            dma((nz, nz, 2)), dma((nz, nz)),
            dma((nz, nz)), dma((nz, nz)),
            dma((nz, nz)), dma((nz, nz)),
            dma((nz, nz)), dma((nz, nz)),
            dma((nz, nhp)), dma((nz, nhp)),
            dma((nz,)), dma((nz,)),
        ],
        compiler_params=pltpu.CompilerParams(
            collective_id=0, has_side_effects=True, vmem_limit_bytes=60 * 1024 * 1024
        ),
        cost_estimate=pl.CostEstimate(
            flops=flops, bytes_accessed=2 * (wo.size + 3 * w_gate.size), transcendentals=0
        ),
    )(
        query, keyval, resid, norm_gain.reshape(nz, 1, cols), expert_ids.T, route_weights.T, wo, w_gate, w_up, w_down
    )


def body(
    resid, query, keyval, wo, norm_gain, w_gate, w_up, w_down, expert_ids, slot_ids, route_weights
):
    args = (resid, query, keyval, wo, norm_gain, w_gate, w_up, w_down, expert_ids, slot_ids, route_weights)
    nz, nx, npair = (lax.axis_size(name) for name in ("expert", "head", "pair"))
    rows = resid.shape[0]
    capacity = 2 * rows * TOPK // (w_gate.shape[0] * nz)
    dense = (
        capacity == rows
        and w_gate.shape[0] == 1
        and nz == nx * npair
        and nx == 2
        and npair == 2
        and query.shape[1] // HEAD_WIDTH == QUERY_HEADS // KEY_VALUE_HEADS
        and rows % (16 * nx * npair) == 0
    )
    return fused_body(*args) if dense else slotted_body(*args)


def solution(mesh):
    return jax.shard_map(
        body,
        mesh=mesh,
        in_specs=(
            P(("groups", "expert"), ("head", "pair")),
            P(("groups", "expert"), ("head", "pair")),
            P(None, ("groups", "expert"), "head"),
            P(("head", "pair"), "expert"),
            P(),
            P("expert", None, ("head", "pair")),
            P("expert", None, ("head", "pair")),
            P("expert", None, ("head", "pair")),
            P(("groups", "expert"), None),
            P(("groups", "expert"), None),
            P(("groups", "expert"), None),
        ),
        out_specs=(
            P(("groups", "expert"), ("head", "pair")),
            P(("groups", "expert"), ("head", "pair")),
        ),
        check_vma=False,
    )
```

```python
import functools
import math

import jax
import jax.numpy as jnp
from jax import lax
from jax.experimental import pallas as pl
from jax.experimental.pallas import tpu as pltpu
from jax.sharding import PartitionSpec as P

D = 4096
QUERY_HEADS = 32
KEY_VALUE_HEADS = 4
HEAD_WIDTH = 128
TOPK = 2


norm_eps = 1e-06


def expert_block(w_gate, w_up, w_down, slot_block):
    gate_val = jnp.einsum("ensd,edf->ensf", slot_block, w_gate, preferred_element_type=jnp.float32)
    up_val = jnp.einsum("ensd,edf->ensf", slot_block, w_up, preferred_element_type=jnp.float32)
    activated = (jax.nn.silu(gate_val) * up_val).astype(jnp.bfloat16)
    all_hidden = lax.all_gather(activated, ("head", "pair"), axis=3, tiled=True)
    return jnp.einsum(
        "ensf,efd->ensd", all_hidden, w_down, preferred_element_type=jnp.float32
    ).astype(jnp.bfloat16)


def slotted_body(
    resid, query, keyval, wo, norm_gain, w_gate, w_up, w_down, expert_ids, slot_ids, route_weights
):
    tok_rows = resid.shape[0]
    feature_cols = resid.shape[1]
    q_local = query.shape[1] // HEAD_WIDTH
    kv_local = keyval.shape[2] // HEAD_WIDTH
    heads_per_group = QUERY_HEADS // KEY_VALUE_HEADS
    query_pos = lax.axis_index("expert") * tok_rows + jnp.arange(tok_rows, dtype=jnp.int32)
    key_head = (
        lax.axis_index("pair") * q_local + jnp.arange(q_local, dtype=jnp.int32)
    ) // heads_per_group
    queries = query.reshape(tok_rows, q_local, HEAD_WIDTH)
    inverse_root = 1.0 / math.sqrt(HEAD_WIDTH)
    shards = lax.all_gather(keyval, "expert", axis=1, tiled=True)
    run_max = jnp.full((tok_rows, q_local), -1e30, jnp.float32)
    count = shards.shape[1]
    keys_here = jnp.take(shards[0].reshape(count, kv_local, HEAD_WIDTH), key_head, axis=1)
    values_here = jnp.take(shards[1].reshape(count, kv_local, HEAD_WIDTH), key_head, axis=1)
    scores = (
        jnp.einsum("thd,uhd->thu", queries, keys_here, preferred_element_type=jnp.float32)
        * inverse_root
    )
    key_pos = jnp.arange(count, dtype=jnp.int32)
    visible = (key_pos[None, :] <= query_pos[:, None])[:, None, :]
    scores = jnp.where(visible, scores, -jnp.inf)
    new_max = jnp.maximum(run_max, jnp.max(scores, axis=2))
    weights = jnp.where(visible, jnp.exp(scores - new_max[:, :, None]), 0.0)
    run_total = jnp.sum(weights, axis=2)
    weighted = jnp.einsum(
        "thu,uhd->thd",
        weights.astype(jnp.bfloat16),
        values_here,
        preferred_element_type=jnp.float32,
    )
    run_max, run_total, weighted = (new_max, run_total, weighted)
    heads_out = (
        (weighted / run_total[:, :, None])
        .astype(jnp.bfloat16)
        .reshape(tok_rows, q_local * HEAD_WIDTH)
    )
    partial_proj = jnp.dot(
        heads_out,
        lax.all_gather(wo, "expert", axis=1, tiled=True),
        preferred_element_type=jnp.float32,
    )
    attn_sum = lax.psum_scatter(
        partial_proj.astype(jnp.bfloat16), ("head", "pair"), scatter_dimension=1, tiled=True
    ).astype(jnp.float32)
    attn_hidden = (resid.astype(jnp.float32) + attn_sum).astype(jnp.bfloat16)
    experts_here = w_gate.shape[0]
    experts_all = experts_here * lax.axis_size("expert")
    capacity = 2 * tok_rows * TOPK // experts_all
    target = expert_ids * capacity + slot_ids
    slot_index = jnp.arange(experts_all * capacity, dtype=jnp.int32)
    placing = jnp.sum(
        (target[None, :, :] == slot_index[:, None, None]).astype(jnp.int32), axis=2
    ).astype(jnp.bfloat16)
    row_floats = attn_hidden.astype(jnp.float32)
    square_sum = lax.psum(jnp.sum(row_floats * row_floats, axis=1), ("head", "pair"))
    mean_square = (square_sum / D)[:, None]
    shard_index = lax.axis_index("head") * lax.axis_size("pair") + lax.axis_index("pair")
    gain_part = lax.dynamic_slice_in_dim(norm_gain, shard_index * feature_cols, feature_cols)
    normed = (row_floats * lax.rsqrt(mean_square + norm_eps) * gain_part).astype(jnp.bfloat16)
    filled = jnp.dot(placing, normed, preferred_element_type=jnp.float32).astype(jnp.bfloat16)
    whole_rows = lax.all_gather(
        lax.all_to_all(
            filled.reshape(experts_all, 1, capacity, normed.shape[1]),
            "expert",
            split_axis=0,
            concat_axis=1,
            tiled=True,
        ),
        ("head", "pair"),
        axis=3,
        tiled=True,
    )
    expert_out = expert_block(w_gate, w_up, w_down, whole_rows)
    returned = lax.all_to_all(expert_out, "expert", split_axis=1, concat_axis=0, tiled=True)
    returned = returned.reshape(experts_all * capacity, feature_cols)
    picked = jnp.take(returned, target.reshape(-1), axis=0).reshape(tok_rows, TOPK, feature_cols)
    expert_mix = jnp.sum(route_weights[:, :, None] * picked.astype(jnp.float32), axis=1).astype(
        jnp.bfloat16
    )
    return (attn_hidden, expert_mix)


MESH = pl.DeviceIdType.MESH


def fused_kernel(
    nz, nx, npair, q_hbm, kv_hbm, resid_hbm, gain_hbm, ids_hbm, rw_hbm, wo_hbm, wg_hbm, wu_hbm, wd_hbm,
    hid_ref, mix_ref,
    gain_ref, ids_ref, rw_ref,
    wo, wgu, wd, kv_all, q_all, ho, pbuf, pin, resid_s, resid_t, xall, act_all, eo, ret,
    w_sem, in_sem, kv_s, kv_r, rs_s, rs_r, rt_s, rt_r, q_s, q_r, p_s, p_r, z_s, z_r, x_s, x_r, c_s, c_r, f_s, f_r,
    a_s, a_r, e_s, e_r,
):
    nhp = nx * npair
    g, z = lax.axis_index("groups"), lax.axis_index("expert")
    x, p = lax.axis_index("head"), lax.axis_index("pair")
    hp = x * npair + p
    rows, cols = q_hbm.shape
    part_rows = rows // nhp
    hidden = wg_hbm.shape[2]
    heads = cols // HEAD_WIDTH
    half = cols // 2
    f32, bf16 = jnp.float32, jnp.bfloat16

    def at(zt, hpt):
        return (g, zt, hpt // npair, lax.rem(hpt, npair))

    def remote(src, dst, ssem, rsem, dev):
        return pltpu.make_async_remote_copy(
            src_ref=src, dst_ref=dst, send_sem=ssem, recv_sem=rsem, device_id=dev, device_id_type=MESH
        )

    def same(ref, ssem, rsem, dev):
        return remote(ref, ref, ssem, rsem, dev)

    def slab(index):
        return pl.ds(pl.multiple_of(index * part_rows, part_rows), part_rows)

    mine = slab(hp)
    z_others = [lax.rem(z + d, nz) for d in range(1, nz)]
    hp_others = [lax.rem(hp + d, nhp) for d in range(1, nhp)]
    right_ok, left_ok = z + 1 < nz, z > 0
    right, left = lax.rem(z + 1, nz), lax.rem(z + nz - 1, nz)
    x_dev = (g, z, 1 - x, p)
    c_dev = (g, z, x, 1 - p)
    hp_x = (1 - x) * npair + p
    hp_c = x * npair + 1 - p
    hp_xc = (1 - x) * npair + 1 - p

    key_cols = pl.ds(pl.multiple_of(p * HEAD_WIDTH, HEAD_WIDTH), HEAD_WIDTH)
    small = [
        pltpu.make_async_copy(kv_hbm.at[:, :, key_cols], kv_all.at[z], in_sem.at[0]),
        pltpu.make_async_copy(q_hbm, q_all.at[z], in_sem.at[1]),
        pltpu.make_async_copy(gain_hbm, gain_ref, in_sem.at[2]),
        pltpu.make_async_copy(ids_hbm, ids_ref, in_sem.at[3]),
        pltpu.make_async_copy(rw_hbm, rw_ref, in_sem.at[4]),
    ]
    weights = [
        pltpu.make_async_copy(wo_hbm, wo, w_sem.at[0]),
        pltpu.make_async_copy(wg_hbm.at[0], wgu.at[:, 0:hidden], w_sem.at[1]),
        pltpu.make_async_copy(wu_hbm.at[0], wgu.at[:, hidden : 2 * hidden], w_sem.at[2]),
        pltpu.make_async_copy(wd_hbm.at[0], wd, w_sem.at[3]),
    ]
    for copy in small + weights:
        copy.start()

    barrier = pltpu.get_barrier_semaphore()
    for dz in range(nz):
        for dh in range(nhp):
            if dz or dh:
                pl.semaphore_signal(
                    barrier,
                    inc=1,
                    device_id=at(lax.rem(z + dz, nz), lax.rem(hp + dh, nhp)),
                    device_id_type=MESH,
                )
    pl.semaphore_wait(barrier, nz * nhp - 1)

    def kv_copy(i):
        return remote(kv_hbm.at[:, :, key_cols], kv_all.at[z], kv_s.at[i], kv_r.at[z], at(z_others[i], hp))

    for i in range(nz - 1):
        kv_copy(i).start()

    def q_copy(b, part, way, dev):
        ref = q_all.at[b, :, part * half : (part + 1) * half]
        return same(ref, q_s.at[b, part, way], q_r.at[b, part], at(dev, hp))

    def q_own(part, way, dev):
        span = slice(part * half, (part + 1) * half)
        return remote(
            q_hbm.at[:, span], q_all.at[z, :, span], q_s.at[z, part, way], q_r.at[z, part], at(dev, hp)
        )

    for part in range(2):
        @pl.when(right_ok)
        def _():
            q_own(part, 0, right).start()

        @pl.when(left_ok)
        def _():
            q_own(part, 1, left).start()

    def resid_copy(i):
        return remote(resid_hbm.at[slab(hp_others[i])], resid_s.at[hp], rs_s.at[i], rs_r.at[hp], at(z, hp_others[i]))

    def resid_wait(j):
        return remote(resid_hbm.at[mine], resid_s.at[j], rs_s.at[0], rs_r.at[j], at(z, j))

    def resid_along(i):
        return remote(resid_s.at[z_others[i]], resid_t.at[z], rt_s.at[i], rt_r.at[z], at(z_others[i], hp))

    own_resid = pltpu.make_async_copy(resid_hbm.at[mine], resid_s.at[hp], in_sem.at[5])
    own_resid.start()
    for i in range(nhp - 1):
        resid_copy(i).start()
    own_resid.wait()
    for other in hp_others:
        resid_wait(other).wait_recv()
    for i in range(nz - 1):
        resid_along(i).start()
    resid_t[z] = resid_s[z]

    for copy in small:
        copy.wait()

    scale = 1.0 / math.sqrt(HEAD_WIDTH)
    lower = lax.broadcasted_iota(jnp.int32, (rows, rows), 1) <= lax.broadcasted_iota(
        jnp.int32, (rows, rows), 0
    )

    def attend(b):
        count = (b + 1) * rows
        keys = kv_all[0 : b + 1, 0].reshape(count, HEAD_WIDTH)
        values = kv_all[0 : b + 1, 1].reshape(count, HEAD_WIDTH)
        for h in range(heads):
            span = slice(h * HEAD_WIDTH, (h + 1) * HEAD_WIDTH)
            scores = lax.dot_general(
                q_all[b, :, span], keys, (((1,), (1,)), ((), ())), preferred_element_type=f32
            )
            scores = scores * scale
            kept = jnp.where(lower, scores[:, b * rows :], -jnp.inf)
            if b:
                kept = jnp.concatenate([scores[:, : b * rows], kept], axis=1)
            probs = jnp.exp(kept - jnp.max(kept, axis=1, keepdims=True))
            total = jnp.sum(probs, axis=1, keepdims=True)
            mixed = jnp.dot(probs.astype(bf16), values, preferred_element_type=f32)
            ho[b, :, span] = (mixed / total).astype(bf16)

    def p_copy(b, i):
        return remote(pbuf.at[b, slab(hp_others[i])], pin.at[b, hp], p_s.at[b, i], p_r.at[b, hp], at(z, hp_others[i]))

    def z_copy(b, e, way, dev):
        return same(xall.at[b, e, mine], z_s.at[b, e, way], z_r.at[b, e], at(dev, hp))

    def x_copy(b, e, owner):
        return same(xall.at[b, e, slab(owner)], x_s.at[b, e], x_r.at[b, e], x_dev)

    def c_copy(b, e, owner):
        return same(xall.at[b, e, slab(owner)], c_s.at[b, e], c_r.at[b, e], c_dev)

    def f_copy(b, e, owner):
        return same(xall.at[b, e, slab(owner)], f_s.at[b, e], f_r.at[b, e], c_dev)

    def a_copy(b, i):
        return remote(act_all.at[b, hp], act_all.at[b, hp], a_s.at[b, i], a_r.at[b, hp], at(z, hp_others[i]))

    def e_copy(b):
        return remote(eo.at[b], ret.at[z], e_s.at[b], e_r.at[z], at(b, hp))

    def project(b):
        pbuf[b] = jnp.dot(ho[b], wo[...], preferred_element_type=f32).astype(bf16)
        for i in range(nhp - 1):
            p_copy(b, i).start()

    def query_hop(d):
        for part in range(2):
            @pl.when(z >= d)
            def _():
                q_copy(z - d, part, 0, right).wait_recv()

            @pl.when(jnp.logical_and(z >= d, right_ok))
            def _():
                q_copy(z - d, part, 0, right).start()

            @pl.when(z + d < nz)
            def _():
                q_copy(z + d, part, 1, left).wait_recv()

            @pl.when(jnp.logical_and(z + d < nz, left_ok))
            def _():
                q_copy(z + d, part, 1, left).start()

    def add_up(b):
        @pl.when(z != b)
        def _():
            remote(resid_s.at[0], resid_t.at[b], rt_s.at[0], rt_r.at[b], at(b, hp)).wait_recv()

        for other in hp_others:
            remote(pbuf.at[b, mine], pin.at[b, other], p_s.at[b, 0], p_r.at[b, other], at(z, other)).wait_recv()
        total = pbuf[b, mine, :].astype(f32)
        for other in hp_others:
            total = total + pin[b, other].astype(f32)
        xall[b, z, mine, :] = (resid_t[b].astype(f32) + total).astype(bf16)

        @pl.when(right_ok)
        def _():
            z_copy(b, z, 0, right).start()

        @pl.when(left_ok)
        def _():
            z_copy(b, z, 1, left).start()

        x_copy(b, z, hp).start()
        c_copy(b, z, hp).start()

    def spread(b, d):
        @pl.when(z >= d)
        def _():
            z_copy(b, z - d, 0, right).wait_recv()

        @pl.when(jnp.logical_and(z >= d, right_ok))
        def _():
            z_copy(b, z - d, 0, right).start()

        @pl.when(z + d < nz)
        def _():
            z_copy(b, z + d, 1, left).wait_recv()

        @pl.when(jnp.logical_and(z + d < nz, left_ok))
        def _():
            z_copy(b, z + d, 1, left).start()

        @pl.when(z >= d)
        def _():
            x_copy(b, z - d, hp).start()
            c_copy(b, z - d, hp).start()

        @pl.when(z + d < nz)
        def _():
            x_copy(b, z + d, hp).start()
            c_copy(b, z + d, hp).start()

    def pass_on(b):
        for e in range(nz):
            x_copy(b, e, hp_x).wait_recv()
            f_copy(b, e, hp_x).start()

    def hidden_units(b):
        for e in range(nz):
            c_copy(b, e, hp_c).wait_recv()
            f_copy(b, e, hp_xc).wait_recv()
        square = jnp.zeros((rows, 1), f32)
        for e in range(nz):
            part = xall[b, e].astype(f32)
            square = square + jnp.sum(part * part, axis=1, keepdims=True)
        root = lax.rsqrt(square / D + norm_eps)
        both = jnp.zeros((rows, 2 * hidden), f32)
        for e in range(nz):
            normed = (xall[b, e].astype(f32) * root * gain_ref[e]).astype(bf16)
            both = both + jnp.dot(normed, wgu[e * cols : (e + 1) * cols, :], preferred_element_type=f32)
        gate, up = both[:, :hidden], both[:, hidden:]
        act_all[b, hp] = (gate / (1.0 + jnp.exp(-gate)) * up).astype(bf16)
        for i in range(nhp - 1):
            a_copy(b, i).start()

    def down(b):
        for other in hp_others:
            ref = act_all.at[b, other]
            remote(ref, ref, a_s.at[b, 0], a_r.at[b, other], at(z, other)).wait_recv()
        total = jnp.zeros((rows, cols), f32)
        for j in range(nhp):
            total = total + jnp.dot(
                act_all[b, j], wd[j * hidden : (j + 1) * hidden, :], preferred_element_type=f32
            )
        eo[b] = total.astype(bf16)

        @pl.when(z != b)
        def _():
            e_copy(b).start()

    order = sorted(range(nz), key=lambda b: max(b, nz - 1 - b))
    first, last = order[: nz // 2], order[nz // 2 :]
    query_hop(1)
    for other in z_others:
        remote(kv_hbm.at[:, :, key_cols], kv_all.at[other], kv_s.at[0], kv_r.at[other], at(other, hp)).wait_recv()
    weights[0].wait()
    near_first = z < nz // 2

    @pl.when(near_first)
    def _():
        attend(first[0])

    @pl.when(jnp.logical_not(near_first))
    def _():
        attend(first[1])

    for d in range(2, nz - 1):
        query_hop(d)

    @pl.when(near_first)
    def _():
        attend(first[1])

    @pl.when(jnp.logical_not(near_first))
    def _():
        attend(first[0])

    for b in first:
        project(b)
    for b in first:
        add_up(b)
    query_hop(nz - 1)
    attend(last[0])
    project(last[0])
    for b in first:
        spread(b, 1)
    attend(last[1])
    project(last[1])
    add_up(last[0])
    for b in first:
        spread(b, 2)
    add_up(last[1])
    spread(last[0], 1)
    for b in first:
        spread(b, 3)
    spread(last[1], 1)
    for b in last:
        spread(b, 2)
    pass_on(first[0])
    for b in last:
        spread(b, nz - 1)
    weights[1].wait()
    weights[2].wait()
    weights[3].wait()
    for i in range(nz + 1):
        if i + 1 < nz:
            pass_on(order[i + 1])
        if i < nz:
            hidden_units(order[i])
        if i >= 1:
            down(order[i - 1])

    hid_ref[...] = xall[z, hp]
    diagonal = lax.broadcasted_iota(jnp.int32, (rows, rows), 0) == lax.broadcasted_iota(
        jnp.int32, (rows, rows), 1
    )

    def route_share(expert):
        shares = jnp.sum(jnp.where(ids_ref[...] == expert, rw_ref[...], 0.0), axis=0, keepdims=True)
        return jnp.sum(jnp.where(diagonal, shares, 0.0), axis=1, keepdims=True)

    mix = route_share(z) * eo[z].astype(f32)
    for other in z_others:
        remote(eo.at[0], ret.at[other], e_s.at[0], e_r.at[other], at(other, hp)).wait_recv()
        mix = mix + route_share(other) * ret[other].astype(f32)
    mix_ref[...] = mix.astype(bf16)

    for i in range(nhp - 1):
        resid_copy(i).wait_send()
    for i in range(nz - 1):
        resid_along(i).wait_send()
        kv_copy(i).wait_send()
    for b in range(nz):
        for part in range(2):
            @pl.when(jnp.logical_and(z >= b, right_ok))
            def _():
                q_copy(b, part, 0, right).wait_send()

            @pl.when(jnp.logical_and(z <= b, left_ok))
            def _():
                q_copy(b, part, 1, left).wait_send()

        for i in range(nhp - 1):
            p_copy(b, i).wait_send()
            a_copy(b, i).wait_send()
        for e in range(nz):
            @pl.when(jnp.logical_and(z >= e, right_ok))
            def _():
                z_copy(b, e, 0, right).wait_send()

            @pl.when(jnp.logical_and(z <= e, left_ok))
            def _():
                z_copy(b, e, 1, left).wait_send()

            x_copy(b, e, hp).wait_send()
            c_copy(b, e, hp).wait_send()
            f_copy(b, e, hp_x).wait_send()

        @pl.when(z != b)
        def _():
            e_copy(b).wait_send()


def fused_body(
    resid, query, keyval, wo, norm_gain, w_gate, w_up, w_down, expert_ids, slot_ids, route_weights
):
    nz, nx, npair = (lax.axis_size(name) for name in ("expert", "head", "pair"))
    nhp = nx * npair
    rows, cols = resid.shape
    part_rows = rows // nhp
    hidden = w_gate.shape[2]
    bf16 = jnp.bfloat16
    dma = pltpu.SemaphoreType.DMA
    vmem = pl.BlockSpec(memory_space=pltpu.VMEM)
    in_hbm = pl.BlockSpec(memory_space=pl.ANY)
    out = jax.ShapeDtypeStruct((rows, cols), bf16)
    tokens = nz * rows
    flops = 2 * tokens * (wo.shape[0] * cols + 2 * w_gate.shape[1] * hidden + w_down.shape[1] * cols)
    return pl.pallas_call(
        functools.partial(fused_kernel, nz, nx, npair),
        out_shape=(out, out),
        in_specs=[in_hbm] * 10,
        out_specs=(vmem, vmem),
        scratch_shapes=[
            pltpu.VMEM((nz, 1, cols), jnp.float32),
            pltpu.VMEM((TOPK, rows), jnp.int32),
            pltpu.VMEM((TOPK, rows), jnp.float32),
            pltpu.VMEM(wo.shape, bf16),
            pltpu.VMEM((w_gate.shape[1], 2 * hidden), bf16),
            pltpu.VMEM(w_down.shape[1:], bf16),
            pltpu.VMEM((nz, 2, rows, HEAD_WIDTH), bf16),
            pltpu.VMEM((nz, rows, cols), bf16),
            pltpu.VMEM((nz, rows, cols), bf16),
            pltpu.VMEM((nz, rows, cols), bf16),
            pltpu.VMEM((nz, nhp, part_rows, cols), bf16),
            pltpu.VMEM((nhp, part_rows, cols), bf16),
            pltpu.VMEM((nz, part_rows, cols), bf16),
            pltpu.VMEM((nz, nz, rows, cols), bf16),
            pltpu.VMEM((nz, nhp, rows, hidden), bf16),
            pltpu.VMEM((nz, rows, cols), bf16),
            pltpu.VMEM((nz, rows, cols), bf16),
            dma((4,)),
            dma((6,)),
            dma((nz,)), dma((nz,)),
            dma((nhp,)), dma((nhp,)),
            dma((nz,)), dma((nz,)),
            dma((nz, 2, 2)), dma((nz, 2)),
            dma((nz, nhp)), dma((nz, nhp)),
            dma((nz, nz, 2)), dma((nz, nz)),
            dma((nz, nz)), dma((nz, nz)),
            dma((nz, nz)), dma((nz, nz)),
            dma((nz, nz)), dma((nz, nz)),
            dma((nz, nhp)), dma((nz, nhp)),
            dma((nz,)), dma((nz,)),
        ],
        compiler_params=pltpu.CompilerParams(
            collective_id=0, has_side_effects=True, vmem_limit_bytes=60 * 1024 * 1024
        ),
        cost_estimate=pl.CostEstimate(
            flops=flops, bytes_accessed=2 * (wo.size + 3 * w_gate.size), transcendentals=0
        ),
    )(
        query, keyval, resid, norm_gain.reshape(nz, 1, cols), expert_ids.T, route_weights.T, wo, w_gate, w_up, w_down
    )


def body(
    resid, query, keyval, wo, norm_gain, w_gate, w_up, w_down, expert_ids, slot_ids, route_weights
):
    args = (resid, query, keyval, wo, norm_gain, w_gate, w_up, w_down, expert_ids, slot_ids, route_weights)
    nz, nx, npair = (lax.axis_size(name) for name in ("expert", "head", "pair"))
    rows = resid.shape[0]
    capacity = 2 * rows * TOPK // (w_gate.shape[0] * nz)
    dense = (
        capacity == rows
        and w_gate.shape[0] == 1
        and nz == nx * npair
        and nx == 2
        and npair == 2
        and query.shape[1] // HEAD_WIDTH == QUERY_HEADS // KEY_VALUE_HEADS
        and rows % (16 * nx * npair) == 0
    )
    return fused_body(*args) if dense else slotted_body(*args)


def solution(mesh):
    return jax.shard_map(
        body,
        mesh=mesh,
        in_specs=(
            P(("groups", "expert"), ("head", "pair")),
            P(("groups", "expert"), ("head", "pair")),
            P(None, ("groups", "expert"), "head"),
            P(("head", "pair"), "expert"),
            P(),
            P("expert", None, ("head", "pair")),
            P("expert", None, ("head", "pair")),
            P("expert", None, ("head", "pair")),
            P(("groups", "expert"), None),
            P(("groups", "expert"), None),
            P(("groups", "expert"), None),
        ),
        out_specs=(
            P(("groups", "expert"), ("head", "pair")),
            P(("groups", "expert"), ("head", "pair")),
        ),
        check_vma=False,
    )
```

```python
import functools
import math

import jax
import jax.numpy as jnp
from jax import lax
from jax.experimental import pallas as pl
from jax.experimental.pallas import tpu as pltpu
from jax.sharding import PartitionSpec as P

D = 4096
QUERY_HEADS = 32
KEY_VALUE_HEADS = 4
HEAD_WIDTH = 128
TOPK = 2


norm_eps = 1e-06


def expert_block(w_gate, w_up, w_down, slot_block):
    gate_val = jnp.einsum("ensd,edf->ensf", slot_block, w_gate, preferred_element_type=jnp.float32)
    up_val = jnp.einsum("ensd,edf->ensf", slot_block, w_up, preferred_element_type=jnp.float32)
    activated = (jax.nn.silu(gate_val) * up_val).astype(jnp.bfloat16)
    all_hidden = lax.all_gather(activated, ("head", "pair"), axis=3, tiled=True)
    return jnp.einsum(
        "ensf,efd->ensd", all_hidden, w_down, preferred_element_type=jnp.float32
    ).astype(jnp.bfloat16)


def slotted_body(
    resid, query, keyval, wo, norm_gain, w_gate, w_up, w_down, expert_ids, slot_ids, route_weights
):
    tok_rows = resid.shape[0]
    feature_cols = resid.shape[1]
    q_local = query.shape[1] // HEAD_WIDTH
    kv_local = keyval.shape[2] // HEAD_WIDTH
    heads_per_group = QUERY_HEADS // KEY_VALUE_HEADS
    query_pos = lax.axis_index("expert") * tok_rows + jnp.arange(tok_rows, dtype=jnp.int32)
    key_head = (
        lax.axis_index("pair") * q_local + jnp.arange(q_local, dtype=jnp.int32)
    ) // heads_per_group
    queries = query.reshape(tok_rows, q_local, HEAD_WIDTH)
    inverse_root = 1.0 / math.sqrt(HEAD_WIDTH)
    shards = lax.all_gather(keyval, "expert", axis=1, tiled=True)
    run_max = jnp.full((tok_rows, q_local), -1e30, jnp.float32)
    count = shards.shape[1]
    keys_here = jnp.take(shards[0].reshape(count, kv_local, HEAD_WIDTH), key_head, axis=1)
    values_here = jnp.take(shards[1].reshape(count, kv_local, HEAD_WIDTH), key_head, axis=1)
    scores = (
        jnp.einsum("thd,uhd->thu", queries, keys_here, preferred_element_type=jnp.float32)
        * inverse_root
    )
    key_pos = jnp.arange(count, dtype=jnp.int32)
    visible = (key_pos[None, :] <= query_pos[:, None])[:, None, :]
    scores = jnp.where(visible, scores, -jnp.inf)
    new_max = jnp.maximum(run_max, jnp.max(scores, axis=2))
    weights = jnp.where(visible, jnp.exp(scores - new_max[:, :, None]), 0.0)
    run_total = jnp.sum(weights, axis=2)
    weighted = jnp.einsum(
        "thu,uhd->thd",
        weights.astype(jnp.bfloat16),
        values_here,
        preferred_element_type=jnp.float32,
    )
    run_max, run_total, weighted = (new_max, run_total, weighted)
    heads_out = (
        (weighted / run_total[:, :, None])
        .astype(jnp.bfloat16)
        .reshape(tok_rows, q_local * HEAD_WIDTH)
    )
    partial_proj = jnp.dot(
        heads_out,
        lax.all_gather(wo, "expert", axis=1, tiled=True),
        preferred_element_type=jnp.float32,
    )
    attn_sum = lax.psum_scatter(
        partial_proj.astype(jnp.bfloat16), ("head", "pair"), scatter_dimension=1, tiled=True
    ).astype(jnp.float32)
    attn_hidden = (resid.astype(jnp.float32) + attn_sum).astype(jnp.bfloat16)
    experts_here = w_gate.shape[0]
    experts_all = experts_here * lax.axis_size("expert")
    capacity = 2 * tok_rows * TOPK // experts_all
    target = expert_ids * capacity + slot_ids
    slot_index = jnp.arange(experts_all * capacity, dtype=jnp.int32)
    placing = jnp.sum(
        (target[None, :, :] == slot_index[:, None, None]).astype(jnp.int32), axis=2
    ).astype(jnp.bfloat16)
    row_floats = attn_hidden.astype(jnp.float32)
    square_sum = lax.psum(jnp.sum(row_floats * row_floats, axis=1), ("head", "pair"))
    mean_square = (square_sum / D)[:, None]
    shard_index = lax.axis_index("head") * lax.axis_size("pair") + lax.axis_index("pair")
    gain_part = lax.dynamic_slice_in_dim(norm_gain, shard_index * feature_cols, feature_cols)
    normed = (row_floats * lax.rsqrt(mean_square + norm_eps) * gain_part).astype(jnp.bfloat16)
    filled = jnp.dot(placing, normed, preferred_element_type=jnp.float32).astype(jnp.bfloat16)
    whole_rows = lax.all_gather(
        lax.all_to_all(
            filled.reshape(experts_all, 1, capacity, normed.shape[1]),
            "expert",
            split_axis=0,
            concat_axis=1,
            tiled=True,
        ),
        ("head", "pair"),
        axis=3,
        tiled=True,
    )
    expert_out = expert_block(w_gate, w_up, w_down, whole_rows)
    returned = lax.all_to_all(expert_out, "expert", split_axis=1, concat_axis=0, tiled=True)
    returned = returned.reshape(experts_all * capacity, feature_cols)
    picked = jnp.take(returned, target.reshape(-1), axis=0).reshape(tok_rows, TOPK, feature_cols)
    expert_mix = jnp.sum(route_weights[:, :, None] * picked.astype(jnp.float32), axis=1).astype(
        jnp.bfloat16
    )
    return (attn_hidden, expert_mix)


MESH = pl.DeviceIdType.MESH


def fused_kernel(
    nz, nx, npair, q_hbm, kv_hbm, resid_hbm, gain_hbm, ids_hbm, rw_hbm, wo_hbm, wg_hbm, wu_hbm, wd_hbm,
    hid_ref, mix_ref,
    gain_ref, ids_ref, rw_ref,
    wo, wgu, wd, kv_all, q_all, ho, pbuf, psum, pin, resid_s, resid_t, xall, act_all, eo, ret,
    w_sem, in_sem, kv_s, kv_r, rs_s, rs_r, rt_s, rt_r, q_s, q_r, p_s, p_r, z_s, z_r, x_s, x_r, c_s, c_r, f_s, f_r,
    a_s, a_r, e_s, e_r,
):
    nhp = nx * npair
    g, z = lax.axis_index("groups"), lax.axis_index("expert")
    x, p = lax.axis_index("head"), lax.axis_index("pair")
    hp = x * npair + p
    rows, cols = q_hbm.shape
    part_rows = rows // nhp
    hidden = wg_hbm.shape[2]
    heads = cols // HEAD_WIDTH
    half = cols // 2
    f32, bf16 = jnp.float32, jnp.bfloat16

    def at(zt, hpt):
        return (g, zt, hpt // npair, lax.rem(hpt, npair))

    def remote(src, dst, ssem, rsem, dev):
        return pltpu.make_async_remote_copy(
            src_ref=src, dst_ref=dst, send_sem=ssem, recv_sem=rsem, device_id=dev, device_id_type=MESH
        )

    def same(ref, ssem, rsem, dev):
        return remote(ref, ref, ssem, rsem, dev)

    def slab(index):
        return pl.ds(pl.multiple_of(index * part_rows, part_rows), part_rows)

    mine = slab(hp)
    z_others = [lax.rem(z + d, nz) for d in range(1, nz)]
    hp_others = [lax.rem(hp + d, nhp) for d in range(1, nhp)]
    right_ok, left_ok = z + 1 < nz, z > 0
    right, left = lax.rem(z + 1, nz), lax.rem(z + nz - 1, nz)
    x_dev = (g, z, 1 - x, p)
    c_dev = (g, z, x, 1 - p)
    hp_x = (1 - x) * npair + p
    hp_c = x * npair + 1 - p
    hp_xc = (1 - x) * npair + 1 - p

    key_cols = pl.ds(pl.multiple_of(p * HEAD_WIDTH, HEAD_WIDTH), HEAD_WIDTH)
    small = [
        pltpu.make_async_copy(kv_hbm.at[:, :, key_cols], kv_all.at[z], in_sem.at[0]),
        pltpu.make_async_copy(q_hbm, q_all.at[z], in_sem.at[1]),
        pltpu.make_async_copy(gain_hbm, gain_ref, in_sem.at[2]),
        pltpu.make_async_copy(ids_hbm, ids_ref, in_sem.at[3]),
        pltpu.make_async_copy(rw_hbm, rw_ref, in_sem.at[4]),
    ]
    weights = [
        pltpu.make_async_copy(wo_hbm, wo, w_sem.at[0]),
        pltpu.make_async_copy(wg_hbm.at[0], wgu.at[:, 0:hidden], w_sem.at[1]),
        pltpu.make_async_copy(wu_hbm.at[0], wgu.at[:, hidden : 2 * hidden], w_sem.at[2]),
        pltpu.make_async_copy(wd_hbm.at[0], wd, w_sem.at[3]),
    ]
    for copy in small + weights:
        copy.start()

    barrier = pltpu.get_barrier_semaphore()
    for dz in range(nz):
        for dh in range(nhp):
            if dz or dh:
                pl.semaphore_signal(
                    barrier,
                    inc=1,
                    device_id=at(lax.rem(z + dz, nz), lax.rem(hp + dh, nhp)),
                    device_id_type=MESH,
                )
    pl.semaphore_wait(barrier, nz * nhp - 1)

    def kv_copy(i):
        return remote(kv_hbm.at[:, :, key_cols], kv_all.at[z], kv_s.at[i], kv_r.at[z], at(z_others[i], hp))

    for i in range(nz - 1):
        kv_copy(i).start()

    def q_copy(b, part, way, dev):
        ref = q_all.at[b, :, part * half : (part + 1) * half]
        return same(ref, q_s.at[b, part, way], q_r.at[b, part], at(dev, hp))

    def q_own(part, way, dev):
        span = slice(part * half, (part + 1) * half)
        return remote(
            q_hbm.at[:, span], q_all.at[z, :, span], q_s.at[z, part, way], q_r.at[z, part], at(dev, hp)
        )

    for part in range(2):
        @pl.when(right_ok)
        def _():
            q_own(part, 0, right).start()

        @pl.when(left_ok)
        def _():
            q_own(part, 1, left).start()

    def resid_copy(i):
        return remote(resid_hbm.at[slab(hp_others[i])], resid_s.at[hp], rs_s.at[i], rs_r.at[hp], at(z, hp_others[i]))

    def resid_wait(j):
        return remote(resid_hbm.at[mine], resid_s.at[j], rs_s.at[0], rs_r.at[j], at(z, j))

    def resid_along(i):
        return remote(resid_s.at[z_others[i]], resid_t.at[z], rt_s.at[i], rt_r.at[z], at(z_others[i], hp))

    own_resid = pltpu.make_async_copy(resid_hbm.at[mine], resid_s.at[hp], in_sem.at[5])
    own_resid.start()
    for i in range(nhp - 1):
        resid_copy(i).start()
    own_resid.wait()
    for other in hp_others:
        resid_wait(other).wait_recv()
    for i in range(nz - 1):
        resid_along(i).start()
    resid_t[z] = resid_s[z]

    for copy in small:
        copy.wait()

    scale = 1.0 / math.sqrt(HEAD_WIDTH)
    stack = heads // 2
    lower = lax.broadcasted_iota(jnp.int32, (rows, rows), 1) <= lax.broadcasted_iota(
        jnp.int32, (rows, rows), 0
    )
    lower = jnp.concatenate([lower] * stack, axis=0)

    def attend(b):
        count = (b + 1) * rows
        keys = kv_all[0 : b + 1, 0].reshape(count, HEAD_WIDTH)
        values = kv_all[0 : b + 1, 1].reshape(count, HEAD_WIDTH)
        for h in range(0, heads, stack):
            spans = [slice(i * HEAD_WIDTH, (i + 1) * HEAD_WIDTH) for i in range(h, h + stack)]
            queries = jnp.concatenate([q_all[b, :, span] for span in spans], axis=0)
            scores = lax.dot_general(queries, keys, (((1,), (1,)), ((), ())), preferred_element_type=f32)
            scores = scores * scale
            kept = jnp.where(lower, scores[:, b * rows :], -jnp.inf)
            if b:
                kept = jnp.concatenate([scores[:, : b * rows], kept], axis=1)
            probs = jnp.exp(kept - jnp.max(kept, axis=1, keepdims=True))
            total = jnp.sum(probs, axis=1, keepdims=True)
            mixed = (jnp.dot(probs.astype(bf16), values, preferred_element_type=f32) / total).astype(bf16)
            for i, span in enumerate(spans):
                ho[b, :, span] = mixed[i * rows : (i + 1) * rows]

    def p_copy(b, i, owner):
        return remote(pbuf.at[b, slab(owner)], pin.at[b, i], p_s.at[b, i], p_r.at[b, i], c_dev)

    def px_copy(b):
        return remote(psum.at[b], pin.at[b, 2], p_s.at[b, 2], p_r.at[b, 2], x_dev)

    def z_copy(b, e, way, dev):
        return same(xall.at[b, e, mine], z_s.at[b, e, way], z_r.at[b, e], at(dev, hp))

    def x_copy(b, e, owner):
        return same(xall.at[b, e, slab(owner)], x_s.at[b, e], x_r.at[b, e], x_dev)

    def c_copy(b, e, owner):
        return same(xall.at[b, e, slab(owner)], c_s.at[b, e], c_r.at[b, e], c_dev)

    def f_copy(b, e, owner):
        return same(xall.at[b, e, slab(owner)], f_s.at[b, e], f_r.at[b, e], c_dev)

    def a_copy(b, i, owner):
        return same(act_all.at[b, owner], a_s.at[b, i], a_r.at[b, i], c_dev if i else x_dev)

    def e_copy(b):
        return remote(eo.at[b], ret.at[z], e_s.at[b], e_r.at[z], at(b, hp))

    def project(b):
        pbuf[b] = jnp.dot(ho[b], wo[...], preferred_element_type=f32).astype(bf16)
        p_copy(b, 0, hp_xc).start()
        p_copy(b, 1, hp_c).start()

    def pair_sum(b):
        p_copy(b, 0, hp_xc).wait_recv()
        psum[b] = (pbuf[b, slab(hp_x), :].astype(f32) + pin[b, 0].astype(f32)).astype(bf16)
        px_copy(b).start()

    def query_hop(d):
        for part in range(2):
            @pl.when(z >= d)
            def _():
                q_copy(z - d, part, 0, right).wait_recv()

            @pl.when(jnp.logical_and(z >= d, right_ok))
            def _():
                q_copy(z - d, part, 0, right).start()

            @pl.when(z + d < nz)
            def _():
                q_copy(z + d, part, 1, left).wait_recv()

            @pl.when(jnp.logical_and(z + d < nz, left_ok))
            def _():
                q_copy(z + d, part, 1, left).start()

    def add_up(b):
        @pl.when(z != b)
        def _():
            remote(resid_s.at[0], resid_t.at[b], rt_s.at[0], rt_r.at[b], at(b, hp)).wait_recv()

        p_copy(b, 1, hp_c).wait_recv()
        px_copy(b).wait_recv()
        total = pbuf[b, mine, :].astype(f32) + pin[b, 1].astype(f32) + pin[b, 2].astype(f32)
        xall[b, z, mine, :] = (resid_t[b].astype(f32) + total).astype(bf16)

        @pl.when(right_ok)
        def _():
            z_copy(b, z, 0, right).start()

        @pl.when(left_ok)
        def _():
            z_copy(b, z, 1, left).start()

        x_copy(b, z, hp).start()
        c_copy(b, z, hp).start()

    def spread(b, d):
        @pl.when(z >= d)
        def _():
            z_copy(b, z - d, 0, right).wait_recv()

        @pl.when(jnp.logical_and(z >= d, right_ok))
        def _():
            z_copy(b, z - d, 0, right).start()

        @pl.when(z + d < nz)
        def _():
            z_copy(b, z + d, 1, left).wait_recv()

        @pl.when(jnp.logical_and(z + d < nz, left_ok))
        def _():
            z_copy(b, z + d, 1, left).start()

        @pl.when(z >= d)
        def _():
            x_copy(b, z - d, hp).start()
            c_copy(b, z - d, hp).start()

        @pl.when(z + d < nz)
        def _():
            x_copy(b, z + d, hp).start()
            c_copy(b, z + d, hp).start()

    def pass_on(b):
        for e in range(nz):
            x_copy(b, e, hp_x).wait_recv()
            f_copy(b, e, hp_x).start()

    def hidden_units(b):
        for e in range(nz):
            c_copy(b, e, hp_c).wait_recv()
            f_copy(b, e, hp_xc).wait_recv()
        square = jnp.zeros((rows, 1), f32)
        for e in range(nz):
            part = xall[b, e].astype(f32)
            square = square + jnp.sum(part * part, axis=1, keepdims=True)
        root = lax.rsqrt(square / D + norm_eps)
        both = jnp.zeros((rows, 2 * hidden), f32)
        for e in range(nz):
            normed = (xall[b, e].astype(f32) * root * gain_ref[e]).astype(bf16)
            both = both + jnp.dot(normed, wgu[e * cols : (e + 1) * cols, :], preferred_element_type=f32)
        gate, up = both[:, :hidden], both[:, hidden:]
        act_all[b, hp] = (gate / (1.0 + jnp.exp(-gate)) * up).astype(bf16)
        a_copy(b, 0, hp).start()
        a_copy(b, 1, hp).start()

    def act_pass(b):
        a_copy(b, 0, hp_x).wait_recv()
        a_copy(b, 2, hp_x).start()

    def down(b):
        a_copy(b, 1, hp_c).wait_recv()
        a_copy(b, 2, hp_xc).wait_recv()
        total = jnp.zeros((rows, cols), f32)
        for j in range(nhp):
            total = total + jnp.dot(
                act_all[b, j], wd[j * hidden : (j + 1) * hidden, :], preferred_element_type=f32
            )
        eo[b] = total.astype(bf16)

        @pl.when(z != b)
        def _():
            e_copy(b).start()

    order = sorted(range(nz), key=lambda b: max(b, nz - 1 - b))
    first, last = order[: nz // 2], order[nz // 2 :]
    query_hop(1)
    for other in z_others:
        remote(kv_hbm.at[:, :, key_cols], kv_all.at[other], kv_s.at[0], kv_r.at[other], at(other, hp)).wait_recv()
    weights[0].wait()
    near_first = z < nz // 2

    @pl.when(near_first)
    def _():
        attend(first[0])

    @pl.when(jnp.logical_not(near_first))
    def _():
        attend(first[1])

    for d in range(2, nz - 1):
        query_hop(d)

    @pl.when(near_first)
    def _():
        attend(first[1])

    @pl.when(jnp.logical_not(near_first))
    def _():
        attend(first[0])

    for b in first:
        project(b)
    for b in first:
        pair_sum(b)
    query_hop(nz - 1)
    attend(last[0])
    project(last[0])
    for b in first:
        add_up(b)
    pair_sum(last[0])
    attend(last[1])
    project(last[1])
    for b in first:
        spread(b, 1)
    add_up(last[0])
    pair_sum(last[1])
    for b in first:
        spread(b, 2)
    add_up(last[1])
    spread(last[0], 1)
    for b in first:
        spread(b, 3)
    spread(last[1], 1)
    spread(last[0], 2)
    pass_on(first[0])
    spread(last[1], 2)
    for b in last:
        spread(b, 3)
    weights[1].wait()
    weights[2].wait()
    weights[3].wait()
    for i in range(nz + 1):
        if i + 1 < nz:
            pass_on(order[i + 1])
        if i < nz:
            hidden_units(order[i])
        if i >= 1:
            down(order[i - 1])
        if i < nz:
            act_pass(order[i])

    hid_ref[...] = xall[z, hp]
    diagonal = lax.broadcasted_iota(jnp.int32, (rows, rows), 0) == lax.broadcasted_iota(
        jnp.int32, (rows, rows), 1
    )

    def route_share(expert):
        shares = jnp.sum(jnp.where(ids_ref[...] == expert, rw_ref[...], 0.0), axis=0, keepdims=True)
        return jnp.sum(jnp.where(diagonal, shares, 0.0), axis=1, keepdims=True)

    mix = route_share(z) * eo[z].astype(f32)
    for other in z_others:
        remote(eo.at[0], ret.at[other], e_s.at[0], e_r.at[other], at(other, hp)).wait_recv()
        mix = mix + route_share(other) * ret[other].astype(f32)
    mix_ref[...] = mix.astype(bf16)

    for i in range(nhp - 1):
        resid_copy(i).wait_send()
    for i in range(nz - 1):
        resid_along(i).wait_send()
        kv_copy(i).wait_send()
    for b in range(nz):
        for part in range(2):
            @pl.when(jnp.logical_and(z >= b, right_ok))
            def _():
                q_copy(b, part, 0, right).wait_send()

            @pl.when(jnp.logical_and(z <= b, left_ok))
            def _():
                q_copy(b, part, 1, left).wait_send()

        p_copy(b, 0, hp_xc).wait_send()
        p_copy(b, 1, hp_c).wait_send()
        px_copy(b).wait_send()
        a_copy(b, 0, hp).wait_send()
        a_copy(b, 1, hp).wait_send()
        a_copy(b, 2, hp_x).wait_send()
        for e in range(nz):
            @pl.when(jnp.logical_and(z >= e, right_ok))
            def _():
                z_copy(b, e, 0, right).wait_send()

            @pl.when(jnp.logical_and(z <= e, left_ok))
            def _():
                z_copy(b, e, 1, left).wait_send()

            x_copy(b, e, hp).wait_send()
            c_copy(b, e, hp).wait_send()
            f_copy(b, e, hp_x).wait_send()

        @pl.when(z != b)
        def _():
            e_copy(b).wait_send()


def fused_body(
    resid, query, keyval, wo, norm_gain, w_gate, w_up, w_down, expert_ids, slot_ids, route_weights
):
    nz, nx, npair = (lax.axis_size(name) for name in ("expert", "head", "pair"))
    nhp = nx * npair
    rows, cols = resid.shape
    part_rows = rows // nhp
    hidden = w_gate.shape[2]
    bf16 = jnp.bfloat16
    dma = pltpu.SemaphoreType.DMA
    vmem = pl.BlockSpec(memory_space=pltpu.VMEM)
    in_hbm = pl.BlockSpec(memory_space=pl.ANY)
    out = jax.ShapeDtypeStruct((rows, cols), bf16)
    tokens = nz * rows
    flops = 2 * tokens * (wo.shape[0] * cols + 2 * w_gate.shape[1] * hidden + w_down.shape[1] * cols)
    return pl.pallas_call(
        functools.partial(fused_kernel, nz, nx, npair),
        out_shape=(out, out),
        in_specs=[in_hbm] * 10,
        out_specs=(vmem, vmem),
        scratch_shapes=[
            pltpu.VMEM((nz, 1, cols), jnp.float32),
            pltpu.VMEM((TOPK, rows), jnp.int32),
            pltpu.VMEM((TOPK, rows), jnp.float32),
            pltpu.VMEM(wo.shape, bf16),
            pltpu.VMEM((w_gate.shape[1], 2 * hidden), bf16),
            pltpu.VMEM(w_down.shape[1:], bf16),
            pltpu.VMEM((nz, 2, rows, HEAD_WIDTH), bf16),
            pltpu.VMEM((nz, rows, cols), bf16),
            pltpu.VMEM((nz, rows, cols), bf16),
            pltpu.VMEM((nz, rows, cols), bf16),
            pltpu.VMEM((nz, part_rows, cols), bf16),
            pltpu.VMEM((nz, 3, part_rows, cols), bf16),
            pltpu.VMEM((nhp, part_rows, cols), bf16),
            pltpu.VMEM((nz, part_rows, cols), bf16),
            pltpu.VMEM((nz, nz, rows, cols), bf16),
            pltpu.VMEM((nz, nhp, rows, hidden), bf16),
            pltpu.VMEM((nz, rows, cols), bf16),
            pltpu.VMEM((nz, rows, cols), bf16),
            dma((4,)),
            dma((6,)),
            dma((nz,)), dma((nz,)),
            dma((nhp,)), dma((nhp,)),
            dma((nz,)), dma((nz,)),
            dma((nz, 2, 2)), dma((nz, 2)),
            dma((nz, 3)), dma((nz, 3)),
            dma((nz, nz, 2)), dma((nz, nz)),
            dma((nz, nz)), dma((nz, nz)),
            dma((nz, nz)), dma((nz, nz)),
            dma((nz, nz)), dma((nz, nz)),
            dma((nz, 3)), dma((nz, 3)),
            dma((nz,)), dma((nz,)),
        ],
        compiler_params=pltpu.CompilerParams(
            collective_id=0, has_side_effects=True, vmem_limit_bytes=60 * 1024 * 1024
        ),
        cost_estimate=pl.CostEstimate(
            flops=flops, bytes_accessed=2 * (wo.size + 3 * w_gate.size), transcendentals=0
        ),
    )(
        query, keyval, resid, norm_gain.reshape(nz, 1, cols), expert_ids.T, route_weights.T, wo, w_gate, w_up, w_down
    )


def body(
    resid, query, keyval, wo, norm_gain, w_gate, w_up, w_down, expert_ids, slot_ids, route_weights
):
    args = (resid, query, keyval, wo, norm_gain, w_gate, w_up, w_down, expert_ids, slot_ids, route_weights)
    nz, nx, npair = (lax.axis_size(name) for name in ("expert", "head", "pair"))
    rows = resid.shape[0]
    capacity = 2 * rows * TOPK // (w_gate.shape[0] * nz)
    dense = (
        capacity == rows
        and w_gate.shape[0] == 1
        and nz == nx * npair
        and nx == 2
        and npair == 2
        and query.shape[1] // HEAD_WIDTH == QUERY_HEADS // KEY_VALUE_HEADS
        and rows % (16 * nx * npair) == 0
    )
    return fused_body(*args) if dense else slotted_body(*args)


def solution(mesh):
    return jax.shard_map(
        body,
        mesh=mesh,
        in_specs=(
            P(("groups", "expert"), ("head", "pair")),
            P(("groups", "expert"), ("head", "pair")),
            P(None, ("groups", "expert"), "head"),
            P(("head", "pair"), "expert"),
            P(),
            P("expert", None, ("head", "pair")),
            P("expert", None, ("head", "pair")),
            P("expert", None, ("head", "pair")),
            P(("groups", "expert"), None),
            P(("groups", "expert"), None),
            P(("groups", "expert"), None),
        ),
        out_specs=(
            P(("groups", "expert"), ("head", "pair")),
            P(("groups", "expert"), ("head", "pair")),
        ),
        check_vma=False,
    )
```

```python
import functools
import math

import jax
import jax.numpy as jnp
from jax import lax
from jax.experimental import pallas as pl
from jax.experimental.pallas import tpu as pltpu
from jax.sharding import PartitionSpec as P

D = 4096
QUERY_HEADS = 32
KEY_VALUE_HEADS = 4
HEAD_WIDTH = 128
TOPK = 2


norm_eps = 1e-06


def expert_block(w_gate, w_up, w_down, slot_block):
    gate_val = jnp.einsum("ensd,edf->ensf", slot_block, w_gate, preferred_element_type=jnp.float32)
    up_val = jnp.einsum("ensd,edf->ensf", slot_block, w_up, preferred_element_type=jnp.float32)
    activated = (jax.nn.silu(gate_val) * up_val).astype(jnp.bfloat16)
    all_hidden = lax.all_gather(activated, ("head", "pair"), axis=3, tiled=True)
    return jnp.einsum(
        "ensf,efd->ensd", all_hidden, w_down, preferred_element_type=jnp.float32
    ).astype(jnp.bfloat16)


def slotted_body(
    resid, query, keyval, wo, norm_gain, w_gate, w_up, w_down, expert_ids, slot_ids, route_weights
):
    tok_rows = resid.shape[0]
    feature_cols = resid.shape[1]
    q_local = query.shape[1] // HEAD_WIDTH
    kv_local = keyval.shape[2] // HEAD_WIDTH
    heads_per_group = QUERY_HEADS // KEY_VALUE_HEADS
    query_pos = lax.axis_index("expert") * tok_rows + jnp.arange(tok_rows, dtype=jnp.int32)
    key_head = (
        lax.axis_index("pair") * q_local + jnp.arange(q_local, dtype=jnp.int32)
    ) // heads_per_group
    queries = query.reshape(tok_rows, q_local, HEAD_WIDTH)
    inverse_root = 1.0 / math.sqrt(HEAD_WIDTH)
    shards = lax.all_gather(keyval, "expert", axis=1, tiled=True)
    run_max = jnp.full((tok_rows, q_local), -1e30, jnp.float32)
    count = shards.shape[1]
    keys_here = jnp.take(shards[0].reshape(count, kv_local, HEAD_WIDTH), key_head, axis=1)
    values_here = jnp.take(shards[1].reshape(count, kv_local, HEAD_WIDTH), key_head, axis=1)
    scores = (
        jnp.einsum("thd,uhd->thu", queries, keys_here, preferred_element_type=jnp.float32)
        * inverse_root
    )
    key_pos = jnp.arange(count, dtype=jnp.int32)
    visible = (key_pos[None, :] <= query_pos[:, None])[:, None, :]
    scores = jnp.where(visible, scores, -jnp.inf)
    new_max = jnp.maximum(run_max, jnp.max(scores, axis=2))
    weights = jnp.where(visible, jnp.exp(scores - new_max[:, :, None]), 0.0)
    run_total = jnp.sum(weights, axis=2)
    weighted = jnp.einsum(
        "thu,uhd->thd",
        weights.astype(jnp.bfloat16),
        values_here,
        preferred_element_type=jnp.float32,
    )
    run_max, run_total, weighted = (new_max, run_total, weighted)
    heads_out = (
        (weighted / run_total[:, :, None])
        .astype(jnp.bfloat16)
        .reshape(tok_rows, q_local * HEAD_WIDTH)
    )
    partial_proj = jnp.dot(
        heads_out,
        lax.all_gather(wo, "expert", axis=1, tiled=True),
        preferred_element_type=jnp.float32,
    )
    attn_sum = lax.psum_scatter(
        partial_proj.astype(jnp.bfloat16), ("head", "pair"), scatter_dimension=1, tiled=True
    ).astype(jnp.float32)
    attn_hidden = (resid.astype(jnp.float32) + attn_sum).astype(jnp.bfloat16)
    experts_here = w_gate.shape[0]
    experts_all = experts_here * lax.axis_size("expert")
    capacity = 2 * tok_rows * TOPK // experts_all
    target = expert_ids * capacity + slot_ids
    slot_index = jnp.arange(experts_all * capacity, dtype=jnp.int32)
    placing = jnp.sum(
        (target[None, :, :] == slot_index[:, None, None]).astype(jnp.int32), axis=2
    ).astype(jnp.bfloat16)
    row_floats = attn_hidden.astype(jnp.float32)
    square_sum = lax.psum(jnp.sum(row_floats * row_floats, axis=1), ("head", "pair"))
    mean_square = (square_sum / D)[:, None]
    shard_index = lax.axis_index("head") * lax.axis_size("pair") + lax.axis_index("pair")
    gain_part = lax.dynamic_slice_in_dim(norm_gain, shard_index * feature_cols, feature_cols)
    normed = (row_floats * lax.rsqrt(mean_square + norm_eps) * gain_part).astype(jnp.bfloat16)
    filled = jnp.dot(placing, normed, preferred_element_type=jnp.float32).astype(jnp.bfloat16)
    whole_rows = lax.all_gather(
        lax.all_to_all(
            filled.reshape(experts_all, 1, capacity, normed.shape[1]),
            "expert",
            split_axis=0,
            concat_axis=1,
            tiled=True,
        ),
        ("head", "pair"),
        axis=3,
        tiled=True,
    )
    expert_out = expert_block(w_gate, w_up, w_down, whole_rows)
    returned = lax.all_to_all(expert_out, "expert", split_axis=1, concat_axis=0, tiled=True)
    returned = returned.reshape(experts_all * capacity, feature_cols)
    picked = jnp.take(returned, target.reshape(-1), axis=0).reshape(tok_rows, TOPK, feature_cols)
    expert_mix = jnp.sum(route_weights[:, :, None] * picked.astype(jnp.float32), axis=1).astype(
        jnp.bfloat16
    )
    return (attn_hidden, expert_mix)


MESH = pl.DeviceIdType.MESH


def fused_kernel(
    nz, nx, npair, q_hbm, kv_hbm, resid_hbm, gain_hbm, ids_hbm, rw_hbm, wo_hbm, wg_hbm, wu_hbm, wd_hbm,
    hid_ref, mix_ref,
    gain_ref, ids_ref, rw_ref,
    wo, wgu, wd, kv_all, q_all, ho, pbuf, psum, pin, resid_s, resid_t, xall, act_all, eo, ret,
    w_sem, in_sem, kv_s, kv_r, rs_s, rs_r, rt_s, rt_r, q_s, q_r, p_s, p_r, z_s, z_r, x_s, x_r, c_s, c_r, f_s, f_r,
    a_s, a_r, e_s, e_r,
):
    nhp = nx * npair
    g, z = lax.axis_index("groups"), lax.axis_index("expert")
    x, p = lax.axis_index("head"), lax.axis_index("pair")
    hp = x * npair + p
    rows, cols = q_hbm.shape
    part_rows = rows // nhp
    hidden = wg_hbm.shape[2]
    heads = cols // HEAD_WIDTH
    half = cols // 2
    f32, bf16 = jnp.float32, jnp.bfloat16

    def at(zt, hpt):
        return (g, zt, hpt // npair, lax.rem(hpt, npair))

    def remote(src, dst, ssem, rsem, dev):
        return pltpu.make_async_remote_copy(
            src_ref=src, dst_ref=dst, send_sem=ssem, recv_sem=rsem, device_id=dev, device_id_type=MESH
        )

    def same(ref, ssem, rsem, dev):
        return remote(ref, ref, ssem, rsem, dev)

    def slab(index):
        return pl.ds(pl.multiple_of(index * part_rows, part_rows), part_rows)

    mine = slab(hp)
    z_others = [lax.rem(z + d, nz) for d in range(1, nz)]
    hp_others = [lax.rem(hp + d, nhp) for d in range(1, nhp)]
    right_ok, left_ok = z + 1 < nz, z > 0
    right, left = lax.rem(z + 1, nz), lax.rem(z + nz - 1, nz)
    x_dev = (g, z, 1 - x, p)
    c_dev = (g, z, x, 1 - p)
    hp_x = (1 - x) * npair + p
    hp_c = x * npair + 1 - p
    hp_xc = (1 - x) * npair + 1 - p

    key_cols = pl.ds(pl.multiple_of(p * HEAD_WIDTH, HEAD_WIDTH), HEAD_WIDTH)
    small = [
        pltpu.make_async_copy(kv_hbm.at[:, :, key_cols], kv_all.at[z], in_sem.at[0]),
        pltpu.make_async_copy(q_hbm, q_all.at[z], in_sem.at[1]),
        pltpu.make_async_copy(gain_hbm, gain_ref, in_sem.at[2]),
        pltpu.make_async_copy(ids_hbm, ids_ref, in_sem.at[3]),
        pltpu.make_async_copy(rw_hbm, rw_ref, in_sem.at[4]),
    ]
    weights = [
        pltpu.make_async_copy(wo_hbm, wo, w_sem.at[0]),
        pltpu.make_async_copy(wg_hbm.at[0], wgu.at[:, 0:hidden], w_sem.at[1]),
        pltpu.make_async_copy(wu_hbm.at[0], wgu.at[:, hidden : 2 * hidden], w_sem.at[2]),
        pltpu.make_async_copy(wd_hbm.at[0], wd, w_sem.at[3]),
    ]
    for copy in small + weights:
        copy.start()

    barrier = pltpu.get_barrier_semaphore()
    for dz in range(nz):
        for dh in range(nhp):
            if dz or dh:
                pl.semaphore_signal(
                    barrier,
                    inc=1,
                    device_id=at(lax.rem(z + dz, nz), lax.rem(hp + dh, nhp)),
                    device_id_type=MESH,
                )
    pl.semaphore_wait(barrier, nz * nhp - 1)

    def kv_copy(i):
        return remote(kv_hbm.at[:, :, key_cols], kv_all.at[z], kv_s.at[i], kv_r.at[z], at(z_others[i], hp))

    for i in range(nz - 1):
        kv_copy(i).start()

    def q_copy(b, part, way, dev):
        ref = q_all.at[b, :, part * half : (part + 1) * half]
        return same(ref, q_s.at[b, part, way], q_r.at[b, part], at(dev, hp))

    def q_own(part, way, dev):
        span = slice(part * half, (part + 1) * half)
        return remote(
            q_hbm.at[:, span], q_all.at[z, :, span], q_s.at[z, part, way], q_r.at[z, part], at(dev, hp)
        )

    for part in range(2):
        @pl.when(right_ok)
        def _():
            q_own(part, 0, right).start()

        @pl.when(left_ok)
        def _():
            q_own(part, 1, left).start()

    def resid_copy(i):
        return remote(resid_hbm.at[slab(hp_others[i])], resid_s.at[hp], rs_s.at[i], rs_r.at[hp], at(z, hp_others[i]))

    def resid_wait(j):
        return remote(resid_hbm.at[mine], resid_s.at[j], rs_s.at[0], rs_r.at[j], at(z, j))

    def resid_along(i):
        return remote(resid_s.at[z_others[i]], resid_t.at[z], rt_s.at[i], rt_r.at[z], at(z_others[i], hp))

    own_resid = pltpu.make_async_copy(resid_hbm.at[mine], resid_s.at[hp], in_sem.at[5])
    own_resid.start()
    for i in range(nhp - 1):
        resid_copy(i).start()
    own_resid.wait()
    for other in hp_others:
        resid_wait(other).wait_recv()
    resid_t[z] = resid_s[z]

    for copy in small:
        copy.wait()

    scale = 1.0 / math.sqrt(HEAD_WIDTH)
    stack = heads // 2
    lower = lax.broadcasted_iota(jnp.int32, (rows, rows), 1) <= lax.broadcasted_iota(
        jnp.int32, (rows, rows), 0
    )
    lower = jnp.concatenate([lower] * stack, axis=0)

    def attend(b):
        count = (b + 1) * rows
        keys = kv_all[0 : b + 1, 0].reshape(count, HEAD_WIDTH)
        values = kv_all[0 : b + 1, 1].reshape(count, HEAD_WIDTH)
        for h in range(0, heads, stack):
            spans = [slice(i * HEAD_WIDTH, (i + 1) * HEAD_WIDTH) for i in range(h, h + stack)]
            queries = jnp.concatenate([q_all[b, :, span] for span in spans], axis=0)
            scores = lax.dot_general(queries, keys, (((1,), (1,)), ((), ())), preferred_element_type=f32)
            scores = scores * scale
            kept = jnp.where(lower, scores[:, b * rows :], -jnp.inf)
            if b:
                kept = jnp.concatenate([scores[:, : b * rows], kept], axis=1)
            probs = jnp.exp(kept - jnp.max(kept, axis=1, keepdims=True))
            total = jnp.sum(probs, axis=1, keepdims=True)
            mixed = (jnp.dot(probs.astype(bf16), values, preferred_element_type=f32) / total).astype(bf16)
            for i, span in enumerate(spans):
                ho[b, :, span] = mixed[i * rows : (i + 1) * rows]

    def p_copy(b, i, owner):
        return remote(pbuf.at[b, slab(owner)], pin.at[b, i], p_s.at[b, i], p_r.at[b, i], c_dev)

    def px_copy(b):
        return remote(psum.at[b], pin.at[b, 2], p_s.at[b, 2], p_r.at[b, 2], x_dev)

    def z_copy(b, i):
        return same(xall.at[b, z, mine], z_s.at[b, i], z_r.at[b, z], at(z_others[i], hp))

    def x_copy(b, e, owner):
        return same(xall.at[b, e, slab(owner)], x_s.at[b, e], x_r.at[b, e], x_dev)

    def c_copy(b, e, owner):
        return same(xall.at[b, e, slab(owner)], c_s.at[b, e], c_r.at[b, e], c_dev)

    def f_copy(b, e, owner):
        return same(xall.at[b, e, slab(owner)], f_s.at[b, e], f_r.at[b, e], c_dev)

    def a_copy(b, i, owner):
        return same(act_all.at[b, owner], a_s.at[b, i], a_r.at[b, i], c_dev if i else x_dev)

    def e_copy(b):
        return remote(eo.at[b], ret.at[z], e_s.at[b], e_r.at[z], at(b, hp))

    def project(b):
        pbuf[b] = jnp.dot(ho[b], wo[...], preferred_element_type=f32).astype(bf16)
        p_copy(b, 0, hp_xc).start()
        p_copy(b, 1, hp_c).start()

    def pair_sum(b):
        p_copy(b, 0, hp_xc).wait_recv()
        psum[b] = (pbuf[b, slab(hp_x), :].astype(f32) + pin[b, 0].astype(f32)).astype(bf16)
        px_copy(b).start()

    def query_hop(d):
        for part in range(2):
            @pl.when(z >= d)
            def _():
                q_copy(z - d, part, 0, right).wait_recv()

            @pl.when(jnp.logical_and(z >= d, right_ok))
            def _():
                q_copy(z - d, part, 0, right).start()

            @pl.when(z + d < nz)
            def _():
                q_copy(z + d, part, 1, left).wait_recv()

            @pl.when(jnp.logical_and(z + d < nz, left_ok))
            def _():
                q_copy(z + d, part, 1, left).start()

    def add_up(b):
        @pl.when(z != b)
        def _():
            remote(resid_s.at[0], resid_t.at[b], rt_s.at[0], rt_r.at[b], at(b, hp)).wait_recv()

        p_copy(b, 1, hp_c).wait_recv()
        px_copy(b).wait_recv()
        total = pbuf[b, mine, :].astype(f32) + pin[b, 1].astype(f32) + pin[b, 2].astype(f32)
        xall[b, z, mine, :] = (resid_t[b].astype(f32) + total).astype(bf16)

        for i in range(nz - 1):
            z_copy(b, i).start()
        x_copy(b, z, hp).start()
        c_copy(b, z, hp).start()

    def spread(b):
        for other in z_others:
            same(xall.at[b, other, mine], z_s.at[b, 0], z_r.at[b, other], at(other, hp)).wait_recv()
            x_copy(b, other, hp).start()
            c_copy(b, other, hp).start()

    def pass_on(b):
        for e in range(nz):
            x_copy(b, e, hp_x).wait_recv()
            f_copy(b, e, hp_x).start()

    def hidden_units(b):
        for e in range(nz):
            c_copy(b, e, hp_c).wait_recv()
            f_copy(b, e, hp_xc).wait_recv()
        square = jnp.zeros((rows, 1), f32)
        for e in range(nz):
            part = xall[b, e].astype(f32)
            square = square + jnp.sum(part * part, axis=1, keepdims=True)
        root = lax.rsqrt(square / D + norm_eps)
        both = jnp.zeros((rows, 2 * hidden), f32)
        for e in range(nz):
            normed = (xall[b, e].astype(f32) * root * gain_ref[e]).astype(bf16)
            both = both + jnp.dot(normed, wgu[e * cols : (e + 1) * cols, :], preferred_element_type=f32)
        gate, up = both[:, :hidden], both[:, hidden:]
        act_all[b, hp] = (gate / (1.0 + jnp.exp(-gate)) * up).astype(bf16)
        a_copy(b, 0, hp).start()
        a_copy(b, 1, hp).start()

    def act_pass(b):
        a_copy(b, 0, hp_x).wait_recv()
        a_copy(b, 2, hp_x).start()

    def down(b):
        a_copy(b, 1, hp_c).wait_recv()
        a_copy(b, 2, hp_xc).wait_recv()
        total = jnp.zeros((rows, cols), f32)
        for j in range(nhp):
            total = total + jnp.dot(
                act_all[b, j], wd[j * hidden : (j + 1) * hidden, :], preferred_element_type=f32
            )
        eo[b] = total.astype(bf16)

        @pl.when(z != b)
        def _():
            e_copy(b).start()

    order = sorted(range(nz), key=lambda b: max(b, nz - 1 - b))
    first, last = order[: nz // 2], order[nz // 2 :]
    query_hop(1)
    for other in z_others:
        remote(kv_hbm.at[:, :, key_cols], kv_all.at[other], kv_s.at[0], kv_r.at[other], at(other, hp)).wait_recv()
    weights[0].wait()
    near_first = z < nz // 2

    @pl.when(near_first)
    def _():
        attend(first[0])

    @pl.when(jnp.logical_not(near_first))
    def _():
        attend(first[1])

    for d in range(2, nz - 1):
        query_hop(d)
    for i in range(nz - 1):
        resid_along(i).start()

    @pl.when(near_first)
    def _():
        attend(first[1])

    @pl.when(jnp.logical_not(near_first))
    def _():
        attend(first[0])

    for b in first:
        project(b)
    for b in first:
        pair_sum(b)
    for b in first:
        add_up(b)
    query_hop(nz - 1)
    attend(last[0])
    project(last[0])
    for b in first:
        spread(b)
    pair_sum(last[0])
    attend(last[1])
    project(last[1])
    add_up(last[0])
    for b in first:
        pass_on(b)
    pair_sum(last[1])
    add_up(last[1])
    weights[1].wait()
    weights[2].wait()
    weights[3].wait()
    hidden_units(first[0])
    spread(last[0])
    act_pass(first[0])
    hidden_units(first[1])
    spread(last[1])
    pass_on(last[0])
    down(first[0])
    act_pass(first[1])
    pass_on(last[1])
    hidden_units(last[0])
    down(first[1])
    act_pass(last[0])
    hidden_units(last[1])
    down(last[0])
    act_pass(last[1])
    down(last[1])

    hid_ref[...] = xall[z, hp]
    diagonal = lax.broadcasted_iota(jnp.int32, (rows, rows), 0) == lax.broadcasted_iota(
        jnp.int32, (rows, rows), 1
    )

    def route_share(expert):
        shares = jnp.sum(jnp.where(ids_ref[...] == expert, rw_ref[...], 0.0), axis=0, keepdims=True)
        return jnp.sum(jnp.where(diagonal, shares, 0.0), axis=1, keepdims=True)

    mix = route_share(z) * eo[z].astype(f32)
    for other in z_others:
        remote(eo.at[0], ret.at[other], e_s.at[0], e_r.at[other], at(other, hp)).wait_recv()
        mix = mix + route_share(other) * ret[other].astype(f32)
    mix_ref[...] = mix.astype(bf16)

    for i in range(nhp - 1):
        resid_copy(i).wait_send()
    for i in range(nz - 1):
        resid_along(i).wait_send()
        kv_copy(i).wait_send()
    for b in range(nz):
        for part in range(2):
            @pl.when(jnp.logical_and(z >= b, right_ok))
            def _():
                q_copy(b, part, 0, right).wait_send()

            @pl.when(jnp.logical_and(z <= b, left_ok))
            def _():
                q_copy(b, part, 1, left).wait_send()

        p_copy(b, 0, hp_xc).wait_send()
        p_copy(b, 1, hp_c).wait_send()
        px_copy(b).wait_send()
        a_copy(b, 0, hp).wait_send()
        a_copy(b, 1, hp).wait_send()
        a_copy(b, 2, hp_x).wait_send()
        for i in range(nz - 1):
            z_copy(b, i).wait_send()
        for e in range(nz):
            x_copy(b, e, hp).wait_send()
            c_copy(b, e, hp).wait_send()
            f_copy(b, e, hp_x).wait_send()

        @pl.when(z != b)
        def _():
            e_copy(b).wait_send()


def fused_body(
    resid, query, keyval, wo, norm_gain, w_gate, w_up, w_down, expert_ids, slot_ids, route_weights
):
    nz, nx, npair = (lax.axis_size(name) for name in ("expert", "head", "pair"))
    nhp = nx * npair
    rows, cols = resid.shape
    part_rows = rows // nhp
    hidden = w_gate.shape[2]
    bf16 = jnp.bfloat16
    dma = pltpu.SemaphoreType.DMA
    vmem = pl.BlockSpec(memory_space=pltpu.VMEM)
    in_hbm = pl.BlockSpec(memory_space=pl.ANY)
    out = jax.ShapeDtypeStruct((rows, cols), bf16)
    tokens = nz * rows
    flops = 2 * tokens * (wo.shape[0] * cols + 2 * w_gate.shape[1] * hidden + w_down.shape[1] * cols)
    return pl.pallas_call(
        functools.partial(fused_kernel, nz, nx, npair),
        out_shape=(out, out),
        in_specs=[in_hbm] * 10,
        out_specs=(vmem, vmem),
        scratch_shapes=[
            pltpu.VMEM((nz, 1, cols), jnp.float32),
            pltpu.VMEM((TOPK, rows), jnp.int32),
            pltpu.VMEM((TOPK, rows), jnp.float32),
            pltpu.VMEM(wo.shape, bf16),
            pltpu.VMEM((w_gate.shape[1], 2 * hidden), bf16),
            pltpu.VMEM(w_down.shape[1:], bf16),
            pltpu.VMEM((nz, 2, rows, HEAD_WIDTH), bf16),
            pltpu.VMEM((nz, rows, cols), bf16),
            pltpu.VMEM((nz, rows, cols), bf16),
            pltpu.VMEM((nz, rows, cols), bf16),
            pltpu.VMEM((nz, part_rows, cols), bf16),
            pltpu.VMEM((nz, 3, part_rows, cols), bf16),
            pltpu.VMEM((nhp, part_rows, cols), bf16),
            pltpu.VMEM((nz, part_rows, cols), bf16),
            pltpu.VMEM((nz, nz, rows, cols), bf16),
            pltpu.VMEM((nz, nhp, rows, hidden), bf16),
            pltpu.VMEM((nz, rows, cols), bf16),
            pltpu.VMEM((nz, rows, cols), bf16),
            dma((4,)),
            dma((6,)),
            dma((nz,)), dma((nz,)),
            dma((nhp,)), dma((nhp,)),
            dma((nz,)), dma((nz,)),
            dma((nz, 2, 2)), dma((nz, 2)),
            dma((nz, 3)), dma((nz, 3)),
            dma((nz, nz)), dma((nz, nz)),
            dma((nz, nz)), dma((nz, nz)),
            dma((nz, nz)), dma((nz, nz)),
            dma((nz, nz)), dma((nz, nz)),
            dma((nz, 3)), dma((nz, 3)),
            dma((nz,)), dma((nz,)),
        ],
        compiler_params=pltpu.CompilerParams(
            collective_id=0, has_side_effects=True, vmem_limit_bytes=60 * 1024 * 1024
        ),
        cost_estimate=pl.CostEstimate(
            flops=flops, bytes_accessed=2 * (wo.size + 3 * w_gate.size), transcendentals=0
        ),
    )(
        query, keyval, resid, norm_gain.reshape(nz, 1, cols), expert_ids.T, route_weights.T, wo, w_gate, w_up, w_down
    )


def body(
    resid, query, keyval, wo, norm_gain, w_gate, w_up, w_down, expert_ids, slot_ids, route_weights
):
    args = (resid, query, keyval, wo, norm_gain, w_gate, w_up, w_down, expert_ids, slot_ids, route_weights)
    nz, nx, npair = (lax.axis_size(name) for name in ("expert", "head", "pair"))
    rows = resid.shape[0]
    capacity = 2 * rows * TOPK // (w_gate.shape[0] * nz)
    dense = (
        capacity == rows
        and w_gate.shape[0] == 1
        and nz == nx * npair
        and nx == 2
        and npair == 2
        and query.shape[1] // HEAD_WIDTH == QUERY_HEADS // KEY_VALUE_HEADS
        and rows % (16 * nx * npair) == 0
    )
    return fused_body(*args) if dense else slotted_body(*args)


def solution(mesh):
    return jax.shard_map(
        body,
        mesh=mesh,
        in_specs=(
            P(("groups", "expert"), ("head", "pair")),
            P(("groups", "expert"), ("head", "pair")),
            P(None, ("groups", "expert"), "head"),
            P(("head", "pair"), "expert"),
            P(),
            P("expert", None, ("head", "pair")),
            P("expert", None, ("head", "pair")),
            P("expert", None, ("head", "pair")),
            P(("groups", "expert"), None),
            P(("groups", "expert"), None),
            P(("groups", "expert"), None),
        ),
        out_specs=(
            P(("groups", "expert"), ("head", "pair")),
            P(("groups", "expert"), ("head", "pair")),
        ),
        check_vma=False,
    )
```

```python
import functools
import math

import jax
import jax.numpy as jnp
from jax import lax
from jax.experimental import pallas as pl
from jax.experimental.pallas import tpu as pltpu
from jax.sharding import PartitionSpec as P

D = 4096
QUERY_HEADS = 32
KEY_VALUE_HEADS = 4
HEAD_WIDTH = 128
TOPK = 2


norm_eps = 1e-06


def expert_block(w_gate, w_up, w_down, slot_block):
    gate_val = jnp.einsum("ensd,edf->ensf", slot_block, w_gate, preferred_element_type=jnp.float32)
    up_val = jnp.einsum("ensd,edf->ensf", slot_block, w_up, preferred_element_type=jnp.float32)
    activated = (jax.nn.silu(gate_val) * up_val).astype(jnp.bfloat16)
    all_hidden = lax.all_gather(activated, ("head", "pair"), axis=3, tiled=True)
    return jnp.einsum(
        "ensf,efd->ensd", all_hidden, w_down, preferred_element_type=jnp.float32
    ).astype(jnp.bfloat16)


def slotted_body(
    resid, query, keyval, wo, norm_gain, w_gate, w_up, w_down, expert_ids, slot_ids, route_weights
):
    tok_rows = resid.shape[0]
    feature_cols = resid.shape[1]
    q_local = query.shape[1] // HEAD_WIDTH
    kv_local = keyval.shape[2] // HEAD_WIDTH
    heads_per_group = QUERY_HEADS // KEY_VALUE_HEADS
    query_pos = lax.axis_index("expert") * tok_rows + jnp.arange(tok_rows, dtype=jnp.int32)
    key_head = (
        lax.axis_index("pair") * q_local + jnp.arange(q_local, dtype=jnp.int32)
    ) // heads_per_group
    queries = query.reshape(tok_rows, q_local, HEAD_WIDTH)
    inverse_root = 1.0 / math.sqrt(HEAD_WIDTH)
    shards = lax.all_gather(keyval, "expert", axis=1, tiled=True)
    run_max = jnp.full((tok_rows, q_local), -1e30, jnp.float32)
    count = shards.shape[1]
    keys_here = jnp.take(shards[0].reshape(count, kv_local, HEAD_WIDTH), key_head, axis=1)
    values_here = jnp.take(shards[1].reshape(count, kv_local, HEAD_WIDTH), key_head, axis=1)
    scores = (
        jnp.einsum("thd,uhd->thu", queries, keys_here, preferred_element_type=jnp.float32)
        * inverse_root
    )
    key_pos = jnp.arange(count, dtype=jnp.int32)
    visible = (key_pos[None, :] <= query_pos[:, None])[:, None, :]
    scores = jnp.where(visible, scores, -jnp.inf)
    new_max = jnp.maximum(run_max, jnp.max(scores, axis=2))
    weights = jnp.where(visible, jnp.exp(scores - new_max[:, :, None]), 0.0)
    run_total = jnp.sum(weights, axis=2)
    weighted = jnp.einsum(
        "thu,uhd->thd",
        weights.astype(jnp.bfloat16),
        values_here,
        preferred_element_type=jnp.float32,
    )
    run_max, run_total, weighted = (new_max, run_total, weighted)
    heads_out = (
        (weighted / run_total[:, :, None])
        .astype(jnp.bfloat16)
        .reshape(tok_rows, q_local * HEAD_WIDTH)
    )
    partial_proj = jnp.dot(
        heads_out,
        lax.all_gather(wo, "expert", axis=1, tiled=True),
        preferred_element_type=jnp.float32,
    )
    attn_sum = lax.psum_scatter(
        partial_proj.astype(jnp.bfloat16), ("head", "pair"), scatter_dimension=1, tiled=True
    ).astype(jnp.float32)
    attn_hidden = (resid.astype(jnp.float32) + attn_sum).astype(jnp.bfloat16)
    experts_here = w_gate.shape[0]
    experts_all = experts_here * lax.axis_size("expert")
    capacity = 2 * tok_rows * TOPK // experts_all
    target = expert_ids * capacity + slot_ids
    slot_index = jnp.arange(experts_all * capacity, dtype=jnp.int32)
    placing = jnp.sum(
        (target[None, :, :] == slot_index[:, None, None]).astype(jnp.int32), axis=2
    ).astype(jnp.bfloat16)
    row_floats = attn_hidden.astype(jnp.float32)
    square_sum = lax.psum(jnp.sum(row_floats * row_floats, axis=1), ("head", "pair"))
    mean_square = (square_sum / D)[:, None]
    shard_index = lax.axis_index("head") * lax.axis_size("pair") + lax.axis_index("pair")
    gain_part = lax.dynamic_slice_in_dim(norm_gain, shard_index * feature_cols, feature_cols)
    normed = (row_floats * lax.rsqrt(mean_square + norm_eps) * gain_part).astype(jnp.bfloat16)
    filled = jnp.dot(placing, normed, preferred_element_type=jnp.float32).astype(jnp.bfloat16)
    whole_rows = lax.all_gather(
        lax.all_to_all(
            filled.reshape(experts_all, 1, capacity, normed.shape[1]),
            "expert",
            split_axis=0,
            concat_axis=1,
            tiled=True,
        ),
        ("head", "pair"),
        axis=3,
        tiled=True,
    )
    expert_out = expert_block(w_gate, w_up, w_down, whole_rows)
    returned = lax.all_to_all(expert_out, "expert", split_axis=1, concat_axis=0, tiled=True)
    returned = returned.reshape(experts_all * capacity, feature_cols)
    picked = jnp.take(returned, target.reshape(-1), axis=0).reshape(tok_rows, TOPK, feature_cols)
    expert_mix = jnp.sum(route_weights[:, :, None] * picked.astype(jnp.float32), axis=1).astype(
        jnp.bfloat16
    )
    return (attn_hidden, expert_mix)


MESH = pl.DeviceIdType.MESH


def fused_kernel(
    nz, nx, npair, q_hbm, kv_hbm, resid_hbm, gain_hbm, ids_hbm, rw_hbm, wo_hbm, wg_hbm, wu_hbm, wd_hbm,
    hid_ref, mix_ref,
    gain_ref, ids_ref, rw_ref,
    wo, wgu, wd, kv_all, q_all, ho, pbuf, psum, pin, resid_s, resid_t, xall, act_all, eo, ret,
    w_sem, in_sem, kv_s, kv_r, rs_s, rs_r, rt_s, rt_r, q_s, q_r, p_s, p_r, z_s, z_r, x_s, x_r, c_s, c_r, f_s, f_r,
    a_s, a_r, e_s, e_r,
):
    nhp = nx * npair
    g, z = lax.axis_index("groups"), lax.axis_index("expert")
    x, p = lax.axis_index("head"), lax.axis_index("pair")
    hp = x * npair + p
    rows, cols = q_hbm.shape
    part_rows = rows // nhp
    hidden = wg_hbm.shape[2]
    heads = cols // HEAD_WIDTH
    half = cols // 2
    f32, bf16 = jnp.float32, jnp.bfloat16

    def at(zt, hpt):
        return (g, zt, hpt // npair, lax.rem(hpt, npair))

    def remote(src, dst, ssem, rsem, dev):
        return pltpu.make_async_remote_copy(
            src_ref=src, dst_ref=dst, send_sem=ssem, recv_sem=rsem, device_id=dev, device_id_type=MESH
        )

    def same(ref, ssem, rsem, dev):
        return remote(ref, ref, ssem, rsem, dev)

    def slab(index):
        return pl.ds(pl.multiple_of(index * part_rows, part_rows), part_rows)

    mine = slab(hp)
    z_others = [lax.rem(z + d, nz) for d in range(1, nz)]
    hp_others = [lax.rem(hp + d, nhp) for d in range(1, nhp)]
    right_ok, left_ok = z + 1 < nz, z > 0
    right, left = lax.rem(z + 1, nz), lax.rem(z + nz - 1, nz)
    x_dev = (g, z, 1 - x, p)
    c_dev = (g, z, x, 1 - p)
    hp_x = (1 - x) * npair + p
    hp_c = x * npair + 1 - p
    hp_xc = (1 - x) * npair + 1 - p

    key_cols = pl.ds(pl.multiple_of(p * HEAD_WIDTH, HEAD_WIDTH), HEAD_WIDTH)
    small = [
        pltpu.make_async_copy(kv_hbm.at[:, :, key_cols], kv_all.at[z], in_sem.at[0]),
        pltpu.make_async_copy(q_hbm, q_all.at[z], in_sem.at[1]),
        pltpu.make_async_copy(gain_hbm, gain_ref, in_sem.at[2]),
        pltpu.make_async_copy(ids_hbm, ids_ref, in_sem.at[3]),
        pltpu.make_async_copy(rw_hbm, rw_ref, in_sem.at[4]),
    ]
    weights = [
        pltpu.make_async_copy(wo_hbm, wo, w_sem.at[0]),
        pltpu.make_async_copy(wg_hbm.at[0], wgu.at[:, 0:hidden], w_sem.at[1]),
        pltpu.make_async_copy(wu_hbm.at[0], wgu.at[:, hidden : 2 * hidden], w_sem.at[2]),
        pltpu.make_async_copy(wd_hbm.at[0], wd, w_sem.at[3]),
    ]
    for copy in small + weights:
        copy.start()

    barrier = pltpu.get_barrier_semaphore()
    for dz in range(nz):
        for dh in range(nhp):
            if dz or dh:
                pl.semaphore_signal(
                    barrier,
                    inc=1,
                    device_id=at(lax.rem(z + dz, nz), lax.rem(hp + dh, nhp)),
                    device_id_type=MESH,
                )
    pl.semaphore_wait(barrier, nz * nhp - 1)

    def kv_copy(i):
        return remote(kv_hbm.at[:, :, key_cols], kv_all.at[z], kv_s.at[i], kv_r.at[z], at(z_others[i], hp))

    for i in range(nz - 1):
        kv_copy(i).start()

    def q_copy(b, part, way, dev):
        ref = q_all.at[b, :, part * half : (part + 1) * half]
        return same(ref, q_s.at[b, part, way], q_r.at[b, part], at(dev, hp))

    def q_own(part, way, dev):
        span = slice(part * half, (part + 1) * half)
        return remote(
            q_hbm.at[:, span], q_all.at[z, :, span], q_s.at[z, part, way], q_r.at[z, part], at(dev, hp)
        )

    for part in range(2):
        @pl.when(right_ok)
        def _():
            q_own(part, 0, right).start()

        @pl.when(left_ok)
        def _():
            q_own(part, 1, left).start()

    def resid_copy(i):
        return remote(resid_hbm.at[slab(hp_others[i])], resid_s.at[hp], rs_s.at[i], rs_r.at[hp], at(z, hp_others[i]))

    def resid_wait(j):
        return remote(resid_hbm.at[mine], resid_s.at[j], rs_s.at[0], rs_r.at[j], at(z, j))

    def resid_along(i):
        return remote(resid_s.at[z_others[i]], resid_t.at[z], rt_s.at[i], rt_r.at[z], at(z_others[i], hp))

    own_resid = pltpu.make_async_copy(resid_hbm.at[mine], resid_s.at[hp], in_sem.at[5])
    own_resid.start()
    for i in range(nhp - 1):
        resid_copy(i).start()
    own_resid.wait()
    for other in hp_others:
        resid_wait(other).wait_recv()
    resid_t[z] = resid_s[z]

    for copy in small:
        copy.wait()

    scale = 1.0 / math.sqrt(HEAD_WIDTH)
    stack = heads // 2
    lower = lax.broadcasted_iota(jnp.int32, (rows, rows), 1) <= lax.broadcasted_iota(
        jnp.int32, (rows, rows), 0
    )
    lower = jnp.concatenate([lower] * stack, axis=0)

    def attend(b):
        count = (b + 1) * rows
        keys = kv_all[0 : b + 1, 0].reshape(count, HEAD_WIDTH)
        values = kv_all[0 : b + 1, 1].reshape(count, HEAD_WIDTH)
        for h in range(0, heads, stack):
            spans = [slice(i * HEAD_WIDTH, (i + 1) * HEAD_WIDTH) for i in range(h, h + stack)]
            queries = jnp.concatenate([q_all[b, :, span] for span in spans], axis=0)
            scores = lax.dot_general(queries, keys, (((1,), (1,)), ((), ())), preferred_element_type=f32)
            scores = scores * scale
            kept = jnp.where(lower, scores[:, b * rows :], -jnp.inf)
            if b:
                kept = jnp.concatenate([scores[:, : b * rows], kept], axis=1)
            probs = jnp.exp(kept - jnp.max(kept, axis=1, keepdims=True))
            total = jnp.sum(probs, axis=1, keepdims=True)
            mixed = (jnp.dot(probs.astype(bf16), values, preferred_element_type=f32) / total).astype(bf16)
            for i, span in enumerate(spans):
                ho[b, :, span] = mixed[i * rows : (i + 1) * rows]

    def p_copy(b, i, owner):
        return remote(pbuf.at[b, slab(owner)], pin.at[b, i], p_s.at[b, i], p_r.at[b, i], c_dev)

    def px_copy(b):
        return remote(psum.at[b], pin.at[b, 2], p_s.at[b, 2], p_r.at[b, 2], x_dev)

    def z_copy(b, i):
        return same(xall.at[b, z, mine], z_s.at[b, i], z_r.at[b, z], at(z_others[i], hp))

    def x_copy(b, e, owner):
        return same(xall.at[b, e, slab(owner)], x_s.at[b, e], x_r.at[b, e], x_dev)

    def c_copy(b, e, owner):
        return same(xall.at[b, e, slab(owner)], c_s.at[b, e], c_r.at[b, e], c_dev)

    def f_copy(b, e, owner):
        return same(xall.at[b, e, slab(owner)], f_s.at[b, e], f_r.at[b, e], c_dev)

    def a_copy(b, i, owner):
        return same(act_all.at[b, owner], a_s.at[b, i], a_r.at[b, i], c_dev if i else x_dev)

    def e_copy(b):
        return remote(eo.at[b], ret.at[z], e_s.at[b], e_r.at[z], at(b, hp))

    def project(*blocks):
        shares = jnp.dot(
            jnp.concatenate([ho[b] for b in blocks], axis=0), wo[...], preferred_element_type=f32
        ).astype(bf16)
        for i, b in enumerate(blocks):
            pbuf[b] = shares[i * rows : (i + 1) * rows]
            p_copy(b, 0, hp_xc).start()
            p_copy(b, 1, hp_c).start()

    def pair_sum(b):
        p_copy(b, 0, hp_xc).wait_recv()
        psum[b] = (pbuf[b, slab(hp_x), :].astype(f32) + pin[b, 0].astype(f32)).astype(bf16)
        px_copy(b).start()

    def query_hop(d):
        for part in range(2):
            @pl.when(z >= d)
            def _():
                q_copy(z - d, part, 0, right).wait_recv()

            @pl.when(jnp.logical_and(z >= d, right_ok))
            def _():
                q_copy(z - d, part, 0, right).start()

            @pl.when(z + d < nz)
            def _():
                q_copy(z + d, part, 1, left).wait_recv()

            @pl.when(jnp.logical_and(z + d < nz, left_ok))
            def _():
                q_copy(z + d, part, 1, left).start()

    def add_up(b):
        @pl.when(z != b)
        def _():
            remote(resid_s.at[0], resid_t.at[b], rt_s.at[0], rt_r.at[b], at(b, hp)).wait_recv()

        p_copy(b, 1, hp_c).wait_recv()
        px_copy(b).wait_recv()
        total = pbuf[b, mine, :].astype(f32) + pin[b, 1].astype(f32) + pin[b, 2].astype(f32)
        xall[b, z, mine, :] = (resid_t[b].astype(f32) + total).astype(bf16)

        for i in range(nz - 1):
            z_copy(b, i).start()
        x_copy(b, z, hp).start()
        c_copy(b, z, hp).start()

    def spread(b):
        for other in z_others:
            same(xall.at[b, other, mine], z_s.at[b, 0], z_r.at[b, other], at(other, hp)).wait_recv()
            x_copy(b, other, hp).start()
            c_copy(b, other, hp).start()

    def pass_on(b):
        for e in range(nz):
            x_copy(b, e, hp_x).wait_recv()
            f_copy(b, e, hp_x).start()

    def hidden_units(*blocks):
        roots = []
        for b in blocks:
            square = jnp.zeros((rows, 1), f32)
            for e in range(nz):
                c_copy(b, e, hp_c).wait_recv()
                f_copy(b, e, hp_xc).wait_recv()
                part = xall[b, e].astype(f32)
                square = square + jnp.sum(part * part, axis=1, keepdims=True)
            roots.append(lax.rsqrt(square / D + norm_eps))
        both = jnp.zeros((len(blocks) * rows, 2 * hidden), f32)
        for e in range(nz):
            normed = jnp.concatenate(
                [
                    (xall[b, e].astype(f32) * root * gain_ref[e]).astype(bf16)
                    for b, root in zip(blocks, roots)
                ],
                axis=0,
            )
            both = both + jnp.dot(normed, wgu[e * cols : (e + 1) * cols, :], preferred_element_type=f32)
        gate, up = both[:, :hidden], both[:, hidden:]
        activated = (gate / (1.0 + jnp.exp(-gate)) * up).astype(bf16)
        for i, b in enumerate(blocks):
            act_all[b, hp] = activated[i * rows : (i + 1) * rows]
            a_copy(b, 0, hp).start()
            a_copy(b, 1, hp).start()

    def act_pass(b):
        a_copy(b, 0, hp_x).wait_recv()
        a_copy(b, 2, hp_x).start()

    def down(*blocks):
        for b in blocks:
            a_copy(b, 1, hp_c).wait_recv()
            a_copy(b, 2, hp_xc).wait_recv()
        total = jnp.zeros((len(blocks) * rows, cols), f32)
        for j in range(nhp):
            units = jnp.concatenate([act_all[b, j] for b in blocks], axis=0)
            total = total + jnp.dot(units, wd[j * hidden : (j + 1) * hidden, :], preferred_element_type=f32)
        for i, b in enumerate(blocks):
            eo[b] = total[i * rows : (i + 1) * rows].astype(bf16)

            @pl.when(z != b)
            def _():
                e_copy(b).start()

    order = sorted(range(nz), key=lambda b: max(b, nz - 1 - b))
    first, last = order[: nz // 2], order[nz // 2 :]
    query_hop(1)
    for other in z_others:
        remote(kv_hbm.at[:, :, key_cols], kv_all.at[other], kv_s.at[0], kv_r.at[other], at(other, hp)).wait_recv()
    weights[0].wait()
    near_first = z < nz // 2

    @pl.when(near_first)
    def _():
        attend(first[0])

    @pl.when(jnp.logical_not(near_first))
    def _():
        attend(first[1])

    for d in range(2, nz - 1):
        query_hop(d)
    for i in range(nz - 1):
        resid_along(i).start()

    @pl.when(near_first)
    def _():
        attend(first[1])

    @pl.when(jnp.logical_not(near_first))
    def _():
        attend(first[0])

    project(*first)
    for b in first:
        pair_sum(b)
    for b in first:
        add_up(b)
    query_hop(nz - 1)
    attend(last[0])
    project(last[0])
    for b in first:
        spread(b)
    pair_sum(last[0])
    attend(last[1])
    project(last[1])
    add_up(last[0])
    for b in first:
        pass_on(b)
    pair_sum(last[1])
    add_up(last[1])
    weights[1].wait()
    weights[2].wait()
    weights[3].wait()
    hidden_units(*first)
    for b in last:
        spread(b)
    for b in first:
        act_pass(b)
    down(*first)
    for b in last:
        pass_on(b)
    hidden_units(*last)
    for b in last:
        act_pass(b)
    down(*last)

    hid_ref[...] = xall[z, hp]
    diagonal = lax.broadcasted_iota(jnp.int32, (rows, rows), 0) == lax.broadcasted_iota(
        jnp.int32, (rows, rows), 1
    )

    def route_share(expert):
        shares = jnp.sum(jnp.where(ids_ref[...] == expert, rw_ref[...], 0.0), axis=0, keepdims=True)
        return jnp.sum(jnp.where(diagonal, shares, 0.0), axis=1, keepdims=True)

    mix = route_share(z) * eo[z].astype(f32)
    for other in z_others:
        remote(eo.at[0], ret.at[other], e_s.at[0], e_r.at[other], at(other, hp)).wait_recv()
        mix = mix + route_share(other) * ret[other].astype(f32)
    mix_ref[...] = mix.astype(bf16)

    for i in range(nhp - 1):
        resid_copy(i).wait_send()
    for i in range(nz - 1):
        resid_along(i).wait_send()
        kv_copy(i).wait_send()
    for b in range(nz):
        for part in range(2):
            @pl.when(jnp.logical_and(z >= b, right_ok))
            def _():
                q_copy(b, part, 0, right).wait_send()

            @pl.when(jnp.logical_and(z <= b, left_ok))
            def _():
                q_copy(b, part, 1, left).wait_send()

        p_copy(b, 0, hp_xc).wait_send()
        p_copy(b, 1, hp_c).wait_send()
        px_copy(b).wait_send()
        a_copy(b, 0, hp).wait_send()
        a_copy(b, 1, hp).wait_send()
        a_copy(b, 2, hp_x).wait_send()
        for i in range(nz - 1):
            z_copy(b, i).wait_send()
        for e in range(nz):
            x_copy(b, e, hp).wait_send()
            c_copy(b, e, hp).wait_send()
            f_copy(b, e, hp_x).wait_send()

        @pl.when(z != b)
        def _():
            e_copy(b).wait_send()


def fused_body(
    resid, query, keyval, wo, norm_gain, w_gate, w_up, w_down, expert_ids, slot_ids, route_weights
):
    nz, nx, npair = (lax.axis_size(name) for name in ("expert", "head", "pair"))
    nhp = nx * npair
    rows, cols = resid.shape
    part_rows = rows // nhp
    hidden = w_gate.shape[2]
    bf16 = jnp.bfloat16
    dma = pltpu.SemaphoreType.DMA
    vmem = pl.BlockSpec(memory_space=pltpu.VMEM)
    in_hbm = pl.BlockSpec(memory_space=pl.ANY)
    out = jax.ShapeDtypeStruct((rows, cols), bf16)
    tokens = nz * rows
    flops = 2 * tokens * (wo.shape[0] * cols + 2 * w_gate.shape[1] * hidden + w_down.shape[1] * cols)
    return pl.pallas_call(
        functools.partial(fused_kernel, nz, nx, npair),
        out_shape=(out, out),
        in_specs=[in_hbm] * 10,
        out_specs=(vmem, vmem),
        scratch_shapes=[
            pltpu.VMEM((nz, 1, cols), jnp.float32),
            pltpu.VMEM((TOPK, rows), jnp.int32),
            pltpu.VMEM((TOPK, rows), jnp.float32),
            pltpu.VMEM(wo.shape, bf16),
            pltpu.VMEM((w_gate.shape[1], 2 * hidden), bf16),
            pltpu.VMEM(w_down.shape[1:], bf16),
            pltpu.VMEM((nz, 2, rows, HEAD_WIDTH), bf16),
            pltpu.VMEM((nz, rows, cols), bf16),
            pltpu.VMEM((nz, rows, cols), bf16),
            pltpu.VMEM((nz, rows, cols), bf16),
            pltpu.VMEM((nz, part_rows, cols), bf16),
            pltpu.VMEM((nz, 3, part_rows, cols), bf16),
            pltpu.VMEM((nhp, part_rows, cols), bf16),
            pltpu.VMEM((nz, part_rows, cols), bf16),
            pltpu.VMEM((nz, nz, rows, cols), bf16),
            pltpu.VMEM((nz, nhp, rows, hidden), bf16),
            pltpu.VMEM((nz, rows, cols), bf16),
            pltpu.VMEM((nz, rows, cols), bf16),
            dma((4,)),
            dma((6,)),
            dma((nz,)), dma((nz,)),
            dma((nhp,)), dma((nhp,)),
            dma((nz,)), dma((nz,)),
            dma((nz, 2, 2)), dma((nz, 2)),
            dma((nz, 3)), dma((nz, 3)),
            dma((nz, nz)), dma((nz, nz)),
            dma((nz, nz)), dma((nz, nz)),
            dma((nz, nz)), dma((nz, nz)),
            dma((nz, nz)), dma((nz, nz)),
            dma((nz, 3)), dma((nz, 3)),
            dma((nz,)), dma((nz,)),
        ],
        compiler_params=pltpu.CompilerParams(
            collective_id=0, has_side_effects=True, vmem_limit_bytes=60 * 1024 * 1024
        ),
        cost_estimate=pl.CostEstimate(
            flops=flops, bytes_accessed=2 * (wo.size + 3 * w_gate.size), transcendentals=0
        ),
    )(
        query, keyval, resid, norm_gain.reshape(nz, 1, cols), expert_ids.T, route_weights.T, wo, w_gate, w_up, w_down
    )


def body(
    resid, query, keyval, wo, norm_gain, w_gate, w_up, w_down, expert_ids, slot_ids, route_weights
):
    args = (resid, query, keyval, wo, norm_gain, w_gate, w_up, w_down, expert_ids, slot_ids, route_weights)
    nz, nx, npair = (lax.axis_size(name) for name in ("expert", "head", "pair"))
    rows = resid.shape[0]
    capacity = 2 * rows * TOPK // (w_gate.shape[0] * nz)
    dense = (
        capacity == rows
        and w_gate.shape[0] == 1
        and nz == nx * npair
        and nx == 2
        and npair == 2
        and query.shape[1] // HEAD_WIDTH == QUERY_HEADS // KEY_VALUE_HEADS
        and rows % (16 * nx * npair) == 0
    )
    return fused_body(*args) if dense else slotted_body(*args)


def solution(mesh):
    return jax.shard_map(
        body,
        mesh=mesh,
        in_specs=(
            P(("groups", "expert"), ("head", "pair")),
            P(("groups", "expert"), ("head", "pair")),
            P(None, ("groups", "expert"), "head"),
            P(("head", "pair"), "expert"),
            P(),
            P("expert", None, ("head", "pair")),
            P("expert", None, ("head", "pair")),
            P("expert", None, ("head", "pair")),
            P(("groups", "expert"), None),
            P(("groups", "expert"), None),
            P(("groups", "expert"), None),
        ),
        out_specs=(
            P(("groups", "expert"), ("head", "pair")),
            P(("groups", "expert"), ("head", "pair")),
        ),
        check_vma=False,
    )
```

```python
import functools
import math

import jax
import jax.numpy as jnp
from jax import lax
from jax.experimental import pallas as pl
from jax.experimental.pallas import tpu as pltpu
from jax.sharding import PartitionSpec as P

D = 4096
QUERY_HEADS = 32
KEY_VALUE_HEADS = 4
HEAD_WIDTH = 128
TOPK = 2


norm_eps = 1e-06


def expert_block(w_gate, w_up, w_down, slot_block):
    gate_val = jnp.einsum("ensd,edf->ensf", slot_block, w_gate, preferred_element_type=jnp.float32)
    up_val = jnp.einsum("ensd,edf->ensf", slot_block, w_up, preferred_element_type=jnp.float32)
    activated = (jax.nn.silu(gate_val) * up_val).astype(jnp.bfloat16)
    all_hidden = lax.all_gather(activated, ("head", "pair"), axis=3, tiled=True)
    return jnp.einsum(
        "ensf,efd->ensd", all_hidden, w_down, preferred_element_type=jnp.float32
    ).astype(jnp.bfloat16)


def slotted_body(
    resid, query, keyval, wo, norm_gain, w_gate, w_up, w_down, expert_ids, slot_ids, route_weights
):
    tok_rows = resid.shape[0]
    feature_cols = resid.shape[1]
    q_local = query.shape[1] // HEAD_WIDTH
    kv_local = keyval.shape[2] // HEAD_WIDTH
    heads_per_group = QUERY_HEADS // KEY_VALUE_HEADS
    query_pos = lax.axis_index("expert") * tok_rows + jnp.arange(tok_rows, dtype=jnp.int32)
    key_head = (
        lax.axis_index("pair") * q_local + jnp.arange(q_local, dtype=jnp.int32)
    ) // heads_per_group
    queries = query.reshape(tok_rows, q_local, HEAD_WIDTH)
    inverse_root = 1.0 / math.sqrt(HEAD_WIDTH)
    shards = lax.all_gather(keyval, "expert", axis=1, tiled=True)
    run_max = jnp.full((tok_rows, q_local), -1e30, jnp.float32)
    count = shards.shape[1]
    keys_here = jnp.take(shards[0].reshape(count, kv_local, HEAD_WIDTH), key_head, axis=1)
    values_here = jnp.take(shards[1].reshape(count, kv_local, HEAD_WIDTH), key_head, axis=1)
    scores = (
        jnp.einsum("thd,uhd->thu", queries, keys_here, preferred_element_type=jnp.float32)
        * inverse_root
    )
    key_pos = jnp.arange(count, dtype=jnp.int32)
    visible = (key_pos[None, :] <= query_pos[:, None])[:, None, :]
    scores = jnp.where(visible, scores, -jnp.inf)
    new_max = jnp.maximum(run_max, jnp.max(scores, axis=2))
    weights = jnp.where(visible, jnp.exp(scores - new_max[:, :, None]), 0.0)
    run_total = jnp.sum(weights, axis=2)
    weighted = jnp.einsum(
        "thu,uhd->thd",
        weights.astype(jnp.bfloat16),
        values_here,
        preferred_element_type=jnp.float32,
    )
    run_max, run_total, weighted = (new_max, run_total, weighted)
    heads_out = (
        (weighted / run_total[:, :, None])
        .astype(jnp.bfloat16)
        .reshape(tok_rows, q_local * HEAD_WIDTH)
    )
    partial_proj = jnp.dot(
        heads_out,
        lax.all_gather(wo, "expert", axis=1, tiled=True),
        preferred_element_type=jnp.float32,
    )
    attn_sum = lax.psum_scatter(
        partial_proj.astype(jnp.bfloat16), ("head", "pair"), scatter_dimension=1, tiled=True
    ).astype(jnp.float32)
    attn_hidden = (resid.astype(jnp.float32) + attn_sum).astype(jnp.bfloat16)
    experts_here = w_gate.shape[0]
    experts_all = experts_here * lax.axis_size("expert")
    capacity = 2 * tok_rows * TOPK // experts_all
    target = expert_ids * capacity + slot_ids
    slot_index = jnp.arange(experts_all * capacity, dtype=jnp.int32)
    placing = jnp.sum(
        (target[None, :, :] == slot_index[:, None, None]).astype(jnp.int32), axis=2
    ).astype(jnp.bfloat16)
    row_floats = attn_hidden.astype(jnp.float32)
    square_sum = lax.psum(jnp.sum(row_floats * row_floats, axis=1), ("head", "pair"))
    mean_square = (square_sum / D)[:, None]
    shard_index = lax.axis_index("head") * lax.axis_size("pair") + lax.axis_index("pair")
    gain_part = lax.dynamic_slice_in_dim(norm_gain, shard_index * feature_cols, feature_cols)
    normed = (row_floats * lax.rsqrt(mean_square + norm_eps) * gain_part).astype(jnp.bfloat16)
    filled = jnp.dot(placing, normed, preferred_element_type=jnp.float32).astype(jnp.bfloat16)
    whole_rows = lax.all_gather(
        lax.all_to_all(
            filled.reshape(experts_all, 1, capacity, normed.shape[1]),
            "expert",
            split_axis=0,
            concat_axis=1,
            tiled=True,
        ),
        ("head", "pair"),
        axis=3,
        tiled=True,
    )
    expert_out = expert_block(w_gate, w_up, w_down, whole_rows)
    returned = lax.all_to_all(expert_out, "expert", split_axis=1, concat_axis=0, tiled=True)
    returned = returned.reshape(experts_all * capacity, feature_cols)
    picked = jnp.take(returned, target.reshape(-1), axis=0).reshape(tok_rows, TOPK, feature_cols)
    expert_mix = jnp.sum(route_weights[:, :, None] * picked.astype(jnp.float32), axis=1).astype(
        jnp.bfloat16
    )
    return (attn_hidden, expert_mix)


MESH = pl.DeviceIdType.MESH


def fused_kernel(
    nz, nx, npair, q_hbm, kv_hbm, resid_hbm, gain_hbm, ids_hbm, rw_hbm, wo_hbm, wg_hbm, wu_hbm, wd_hbm,
    hid_ref, mix_ref,
    gain_ref, ids_ref, rw_ref,
    wo, wgu, wd, kv_all, q_all, ho, pbuf, psum, pin, resid_s, resid_t, xall, act_all, eo, ret,
    w_sem, in_sem, kv_s, kv_r, rs_s, rs_r, rt_s, rt_r, q_s, q_r, p_s, p_r, z_s, z_r, x_s, x_r, c_s, c_r, f_s, f_r,
    a_s, a_r, e_s, e_r,
):
    nhp = nx * npair
    g, z = lax.axis_index("groups"), lax.axis_index("expert")
    x, p = lax.axis_index("head"), lax.axis_index("pair")
    hp = x * npair + p
    rows, cols = q_hbm.shape
    part_rows = rows // nhp
    hidden = wg_hbm.shape[2]
    heads = cols // HEAD_WIDTH
    half = cols // 2
    f32, bf16 = jnp.float32, jnp.bfloat16

    def at(zt, hpt):
        return (g, zt, hpt // npair, lax.rem(hpt, npair))

    def remote(src, dst, ssem, rsem, dev):
        return pltpu.make_async_remote_copy(
            src_ref=src, dst_ref=dst, send_sem=ssem, recv_sem=rsem, device_id=dev, device_id_type=MESH
        )

    def same(ref, ssem, rsem, dev):
        return remote(ref, ref, ssem, rsem, dev)

    def slab(index):
        return pl.ds(pl.multiple_of(index * part_rows, part_rows), part_rows)

    mine = slab(hp)
    z_others = [lax.rem(z + d, nz) for d in range(1, nz)]
    hp_others = [lax.rem(hp + d, nhp) for d in range(1, nhp)]
    right_ok, left_ok = z + 1 < nz, z > 0
    right, left = lax.rem(z + 1, nz), lax.rem(z + nz - 1, nz)
    x_dev = (g, z, 1 - x, p)
    c_dev = (g, z, x, 1 - p)
    hp_x = (1 - x) * npair + p
    hp_c = x * npair + 1 - p
    hp_xc = (1 - x) * npair + 1 - p

    key_cols = pl.ds(pl.multiple_of(p * HEAD_WIDTH, HEAD_WIDTH), HEAD_WIDTH)
    small = [
        pltpu.make_async_copy(kv_hbm.at[:, :, key_cols], kv_all.at[z], in_sem.at[0]),
        pltpu.make_async_copy(q_hbm, q_all.at[z], in_sem.at[1]),
        pltpu.make_async_copy(gain_hbm, gain_ref, in_sem.at[2]),
        pltpu.make_async_copy(ids_hbm, ids_ref, in_sem.at[3]),
        pltpu.make_async_copy(rw_hbm, rw_ref, in_sem.at[4]),
    ]
    weights = [
        pltpu.make_async_copy(wo_hbm, wo, w_sem.at[0]),
        pltpu.make_async_copy(wg_hbm.at[0], wgu.at[:, 0:hidden], w_sem.at[1]),
        pltpu.make_async_copy(wu_hbm.at[0], wgu.at[:, hidden : 2 * hidden], w_sem.at[2]),
        pltpu.make_async_copy(wd_hbm.at[0], wd, w_sem.at[3]),
    ]
    for copy in small + weights:
        copy.start()

    barrier = pltpu.get_barrier_semaphore()
    for dz in range(nz):
        for dh in range(nhp):
            if dz or dh:
                pl.semaphore_signal(
                    barrier,
                    inc=1,
                    device_id=at(lax.rem(z + dz, nz), lax.rem(hp + dh, nhp)),
                    device_id_type=MESH,
                )
    pl.semaphore_wait(barrier, nz * nhp - 1)

    def kv_copy(i):
        return remote(kv_hbm.at[:, :, key_cols], kv_all.at[z], kv_s.at[i], kv_r.at[z], at(z_others[i], hp))

    for i in range(nz - 1):
        kv_copy(i).start()

    def q_copy(b, part, way, dev):
        ref = q_all.at[b, :, part * half : (part + 1) * half]
        return same(ref, q_s.at[b, part, way], q_r.at[b, part], at(dev, hp))

    def q_own(part, way, dev):
        span = slice(part * half, (part + 1) * half)
        return remote(
            q_hbm.at[:, span], q_all.at[z, :, span], q_s.at[z, part, way], q_r.at[z, part], at(dev, hp)
        )

    for part in range(2):
        @pl.when(right_ok)
        def _():
            q_own(part, 0, right).start()

        @pl.when(left_ok)
        def _():
            q_own(part, 1, left).start()

    def resid_copy(i):
        return remote(resid_hbm.at[slab(hp_others[i])], resid_s.at[hp], rs_s.at[i], rs_r.at[hp], at(z, hp_others[i]))

    def resid_wait(j):
        return remote(resid_hbm.at[mine], resid_s.at[j], rs_s.at[0], rs_r.at[j], at(z, j))

    def resid_along(i):
        return remote(resid_s.at[z_others[i]], resid_t.at[z], rt_s.at[i], rt_r.at[z], at(z_others[i], hp))

    own_resid = pltpu.make_async_copy(resid_hbm.at[mine], resid_s.at[hp], in_sem.at[5])
    own_resid.start()
    for i in range(nhp - 1):
        resid_copy(i).start()
    own_resid.wait()
    for other in hp_others:
        resid_wait(other).wait_recv()
    resid_t[z] = resid_s[z]

    for copy in small:
        copy.wait()

    scale = 1.0 / math.sqrt(HEAD_WIDTH)
    stack = heads // 2
    lower = lax.broadcasted_iota(jnp.int32, (rows, rows), 1) <= lax.broadcasted_iota(
        jnp.int32, (rows, rows), 0
    )
    lower = jnp.concatenate([lower] * stack, axis=0)

    def attend(b):
        count = (b + 1) * rows
        keys = kv_all[0 : b + 1, 0].reshape(count, HEAD_WIDTH)
        values = kv_all[0 : b + 1, 1].reshape(count, HEAD_WIDTH)
        for h in range(0, heads, stack):
            spans = [slice(i * HEAD_WIDTH, (i + 1) * HEAD_WIDTH) for i in range(h, h + stack)]
            queries = jnp.concatenate([q_all[b, :, span] for span in spans], axis=0)
            scores = lax.dot_general(queries, keys, (((1,), (1,)), ((), ())), preferred_element_type=f32)
            scores = scores * scale
            kept = jnp.where(lower, scores[:, b * rows :], -jnp.inf)
            if b:
                kept = jnp.concatenate([scores[:, : b * rows], kept], axis=1)
            probs = jnp.exp(kept - jnp.max(kept, axis=1, keepdims=True))
            total = jnp.sum(probs, axis=1, keepdims=True)
            mixed = (jnp.dot(probs.astype(bf16), values, preferred_element_type=f32) / total).astype(bf16)
            for i, span in enumerate(spans):
                ho[b, :, span] = mixed[i * rows : (i + 1) * rows]

    def p_copy(b, i, owner):
        return remote(pbuf.at[b, slab(owner)], pin.at[b, i], p_s.at[b, i], p_r.at[b, i], c_dev)

    def px_copy(b):
        return remote(psum.at[b], pin.at[b, 2], p_s.at[b, 2], p_r.at[b, 2], x_dev)

    def z_copy(b, i):
        return same(xall.at[b, z, mine], z_s.at[b, i], z_r.at[b, z], at(z_others[i], hp))

    def x_copy(b, e, owner):
        return same(xall.at[b, e, slab(owner)], x_s.at[b, e], x_r.at[b, e], x_dev)

    def c_copy(b, e, owner):
        return same(xall.at[b, e, slab(owner)], c_s.at[b, e], c_r.at[b, e], c_dev)

    def f_copy(b, e, owner):
        return same(xall.at[b, e, slab(owner)], f_s.at[b, e], f_r.at[b, e], c_dev)

    def a_copy(b, i, owner):
        return same(act_all.at[b, owner], a_s.at[b, i], a_r.at[b, i], c_dev if i else x_dev)

    def e_copy(b):
        return remote(eo.at[b], ret.at[z], e_s.at[b], e_r.at[z], at(b, hp))

    def project(b):
        pbuf[b] = jnp.dot(ho[b], wo[...], preferred_element_type=f32).astype(bf16)
        p_copy(b, 0, hp_xc).start()
        p_copy(b, 1, hp_c).start()

    def pair_sum(b):
        p_copy(b, 0, hp_xc).wait_recv()
        psum[b] = (pbuf[b, slab(hp_x), :].astype(f32) + pin[b, 0].astype(f32)).astype(bf16)
        px_copy(b).start()

    def query_hop(d):
        for part in range(2):
            @pl.when(z >= d)
            def _():
                q_copy(z - d, part, 0, right).wait_recv()

            @pl.when(jnp.logical_and(z >= d, right_ok))
            def _():
                q_copy(z - d, part, 0, right).start()

            @pl.when(z + d < nz)
            def _():
                q_copy(z + d, part, 1, left).wait_recv()

            @pl.when(jnp.logical_and(z + d < nz, left_ok))
            def _():
                q_copy(z + d, part, 1, left).start()

    def add_up(b):
        @pl.when(z != b)
        def _():
            remote(resid_s.at[0], resid_t.at[b], rt_s.at[0], rt_r.at[b], at(b, hp)).wait_recv()

        p_copy(b, 1, hp_c).wait_recv()
        px_copy(b).wait_recv()
        total = pbuf[b, mine, :].astype(f32) + pin[b, 1].astype(f32) + pin[b, 2].astype(f32)
        xall[b, z, mine, :] = (resid_t[b].astype(f32) + total).astype(bf16)

        for i in range(nz - 1):
            z_copy(b, i).start()
        x_copy(b, z, hp).start()
        c_copy(b, z, hp).start()

    def spread(b):
        for other in z_others:
            same(xall.at[b, other, mine], z_s.at[b, 0], z_r.at[b, other], at(other, hp)).wait_recv()
            x_copy(b, other, hp).start()
            c_copy(b, other, hp).start()

    def pass_on(b):
        for e in range(nz):
            x_copy(b, e, hp_x).wait_recv()
            f_copy(b, e, hp_x).start()

    def hidden_units(b):
        for e in range(nz):
            c_copy(b, e, hp_c).wait_recv()
            f_copy(b, e, hp_xc).wait_recv()
        square = jnp.zeros((rows, 1), f32)
        for e in range(nz):
            part = xall[b, e].astype(f32)
            square = square + jnp.sum(part * part, axis=1, keepdims=True)
        root = lax.rsqrt(square / D + norm_eps)
        both = jnp.zeros((rows, 2 * hidden), f32)
        for e in range(nz):
            normed = (xall[b, e].astype(f32) * root * gain_ref[e]).astype(bf16)
            both = both + jnp.dot(normed, wgu[e * cols : (e + 1) * cols, :], preferred_element_type=f32)
        gate, up = both[:, :hidden], both[:, hidden:]
        act_all[b, hp] = (gate / (1.0 + jnp.exp(-gate)) * up).astype(bf16)
        a_copy(b, 0, hp).start()
        a_copy(b, 1, hp).start()

    def act_pass(b):
        a_copy(b, 0, hp_x).wait_recv()
        a_copy(b, 2, hp_x).start()

    def down(b):
        a_copy(b, 1, hp_c).wait_recv()
        a_copy(b, 2, hp_xc).wait_recv()
        total = jnp.zeros((rows, cols), f32)
        for j in range(nhp):
            total = total + jnp.dot(
                act_all[b, j], wd[j * hidden : (j + 1) * hidden, :], preferred_element_type=f32
            )
        eo[b] = total.astype(bf16)

        @pl.when(z != b)
        def _():
            e_copy(b).start()

    order = sorted(range(nz), key=lambda b: max(b, nz - 1 - b))
    first, last = order[: nz // 2], order[nz // 2 :]
    query_hop(1)
    for other in z_others:
        remote(kv_hbm.at[:, :, key_cols], kv_all.at[other], kv_s.at[0], kv_r.at[other], at(other, hp)).wait_recv()
    weights[0].wait()
    near_first = z < nz // 2

    @pl.when(near_first)
    def _():
        attend(first[0])

    @pl.when(jnp.logical_not(near_first))
    def _():
        attend(first[1])

    for d in range(2, nz - 1):
        query_hop(d)
    for i in range(nz - 1):
        resid_along(i).start()

    @pl.when(near_first)
    def _():
        attend(first[1])

    @pl.when(jnp.logical_not(near_first))
    def _():
        attend(first[0])

    for b in first:
        project(b)
    for b in first:
        pair_sum(b)
    for b in first:
        add_up(b)
    query_hop(nz - 1)
    attend(last[0])
    project(last[0])
    for b in first:
        spread(b)
    pair_sum(last[0])
    attend(last[1])
    project(last[1])
    add_up(last[0])
    for b in first:
        pass_on(b)
    pair_sum(last[1])
    add_up(last[1])
    weights[1].wait()
    weights[2].wait()
    weights[3].wait()
    hidden_units(first[0])
    for b in last:
        spread(b)
    act_pass(first[0])
    pass_on(last[0])
    down(first[0])
    pass_on(last[1])
    hidden_units(last[0])
    act_pass(last[0])
    hidden_units(last[1])
    down(last[0])
    act_pass(last[1])
    hidden_units(first[1])
    down(last[1])
    act_pass(first[1])
    down(first[1])

    hid_ref[...] = xall[z, hp]
    diagonal = lax.broadcasted_iota(jnp.int32, (rows, rows), 0) == lax.broadcasted_iota(
        jnp.int32, (rows, rows), 1
    )

    def route_share(expert):
        shares = jnp.sum(jnp.where(ids_ref[...] == expert, rw_ref[...], 0.0), axis=0, keepdims=True)
        return jnp.sum(jnp.where(diagonal, shares, 0.0), axis=1, keepdims=True)

    mix = route_share(z) * eo[z].astype(f32)
    for other in z_others:
        remote(eo.at[0], ret.at[other], e_s.at[0], e_r.at[other], at(other, hp)).wait_recv()
        mix = mix + route_share(other) * ret[other].astype(f32)
    mix_ref[...] = mix.astype(bf16)

    for i in range(nhp - 1):
        resid_copy(i).wait_send()
    for i in range(nz - 1):
        resid_along(i).wait_send()
        kv_copy(i).wait_send()
    for b in range(nz):
        for part in range(2):
            @pl.when(jnp.logical_and(z >= b, right_ok))
            def _():
                q_copy(b, part, 0, right).wait_send()

            @pl.when(jnp.logical_and(z <= b, left_ok))
            def _():
                q_copy(b, part, 1, left).wait_send()

        p_copy(b, 0, hp_xc).wait_send()
        p_copy(b, 1, hp_c).wait_send()
        px_copy(b).wait_send()
        a_copy(b, 0, hp).wait_send()
        a_copy(b, 1, hp).wait_send()
        a_copy(b, 2, hp_x).wait_send()
        for i in range(nz - 1):
            z_copy(b, i).wait_send()
        for e in range(nz):
            x_copy(b, e, hp).wait_send()
            c_copy(b, e, hp).wait_send()
            f_copy(b, e, hp_x).wait_send()

        @pl.when(z != b)
        def _():
            e_copy(b).wait_send()


def fused_body(
    resid, query, keyval, wo, norm_gain, w_gate, w_up, w_down, expert_ids, slot_ids, route_weights
):
    nz, nx, npair = (lax.axis_size(name) for name in ("expert", "head", "pair"))
    nhp = nx * npair
    rows, cols = resid.shape
    part_rows = rows // nhp
    hidden = w_gate.shape[2]
    bf16 = jnp.bfloat16
    dma = pltpu.SemaphoreType.DMA
    vmem = pl.BlockSpec(memory_space=pltpu.VMEM)
    in_hbm = pl.BlockSpec(memory_space=pl.ANY)
    out = jax.ShapeDtypeStruct((rows, cols), bf16)
    tokens = nz * rows
    flops = 2 * tokens * (wo.shape[0] * cols + 2 * w_gate.shape[1] * hidden + w_down.shape[1] * cols)
    return pl.pallas_call(
        functools.partial(fused_kernel, nz, nx, npair),
        out_shape=(out, out),
        in_specs=[in_hbm] * 10,
        out_specs=(vmem, vmem),
        scratch_shapes=[
            pltpu.VMEM((nz, 1, cols), jnp.float32),
            pltpu.VMEM((TOPK, rows), jnp.int32),
            pltpu.VMEM((TOPK, rows), jnp.float32),
            pltpu.VMEM(wo.shape, bf16),
            pltpu.VMEM((w_gate.shape[1], 2 * hidden), bf16),
            pltpu.VMEM(w_down.shape[1:], bf16),
            pltpu.VMEM((nz, 2, rows, HEAD_WIDTH), bf16),
            pltpu.VMEM((nz, rows, cols), bf16),
            pltpu.VMEM((nz, rows, cols), bf16),
            pltpu.VMEM((nz, rows, cols), bf16),
            pltpu.VMEM((nz, part_rows, cols), bf16),
            pltpu.VMEM((nz, 3, part_rows, cols), bf16),
            pltpu.VMEM((nhp, part_rows, cols), bf16),
            pltpu.VMEM((nz, part_rows, cols), bf16),
            pltpu.VMEM((nz, nz, rows, cols), bf16),
            pltpu.VMEM((nz, nhp, rows, hidden), bf16),
            pltpu.VMEM((nz, rows, cols), bf16),
            pltpu.VMEM((nz, rows, cols), bf16),
            dma((4,)),
            dma((6,)),
            dma((nz,)), dma((nz,)),
            dma((nhp,)), dma((nhp,)),
            dma((nz,)), dma((nz,)),
            dma((nz, 2, 2)), dma((nz, 2)),
            dma((nz, 3)), dma((nz, 3)),
            dma((nz, nz)), dma((nz, nz)),
            dma((nz, nz)), dma((nz, nz)),
            dma((nz, nz)), dma((nz, nz)),
            dma((nz, nz)), dma((nz, nz)),
            dma((nz, 3)), dma((nz, 3)),
            dma((nz,)), dma((nz,)),
        ],
        compiler_params=pltpu.CompilerParams(
            collective_id=0, has_side_effects=True, vmem_limit_bytes=60 * 1024 * 1024
        ),
        cost_estimate=pl.CostEstimate(
            flops=flops, bytes_accessed=2 * (wo.size + 3 * w_gate.size), transcendentals=0
        ),
    )(
        query, keyval, resid, norm_gain.reshape(nz, 1, cols), expert_ids.T, route_weights.T, wo, w_gate, w_up, w_down
    )


def body(
    resid, query, keyval, wo, norm_gain, w_gate, w_up, w_down, expert_ids, slot_ids, route_weights
):
    args = (resid, query, keyval, wo, norm_gain, w_gate, w_up, w_down, expert_ids, slot_ids, route_weights)
    nz, nx, npair = (lax.axis_size(name) for name in ("expert", "head", "pair"))
    rows = resid.shape[0]
    capacity = 2 * rows * TOPK // (w_gate.shape[0] * nz)
    dense = (
        capacity == rows
        and w_gate.shape[0] == 1
        and nz == nx * npair
        and nx == 2
        and npair == 2
        and query.shape[1] // HEAD_WIDTH == QUERY_HEADS // KEY_VALUE_HEADS
        and rows % (16 * nx * npair) == 0
    )
    return fused_body(*args) if dense else slotted_body(*args)


def solution(mesh):
    return jax.shard_map(
        body,
        mesh=mesh,
        in_specs=(
            P(("groups", "expert"), ("head", "pair")),
            P(("groups", "expert"), ("head", "pair")),
            P(None, ("groups", "expert"), "head"),
            P(("head", "pair"), "expert"),
            P(),
            P("expert", None, ("head", "pair")),
            P("expert", None, ("head", "pair")),
            P("expert", None, ("head", "pair")),
            P(("groups", "expert"), None),
            P(("groups", "expert"), None),
            P(("groups", "expert"), None),
        ),
        out_specs=(
            P(("groups", "expert"), ("head", "pair")),
            P(("groups", "expert"), ("head", "pair")),
        ),
        check_vma=False,
    )
```
